32 devices in a mesh: grp: 2 (over core), seq: 4 (over y, x), tp: 4 (over z).
Axes of the slice: x: 2, y: 2, z: 4, core: 2. Of those that a mesh axis runs over, the one named last changes fastest.
Arguments:
- prompt: bfloat16 [4096, 8192], P(('grp', 'seq'), 'tp'), may hold values from -6 to 6
- w_kv: bfloat16 [8192, 2048], P(None, 'tp'), may hold values from -0.0625 to 0.0625
- block_owner: int32 [512, 1], P(('grp', 'seq')), may hold values from 0 to 7, as said below
- block_row: int32 [512], P(('grp', 'seq')), may hold values from 0 to 31, as said below
- queries: bfloat16 [256, 4, 8192], P(('grp', 'seq'), None, 'tp'), may hold values from -150 to 150
- new_kv: bfloat16 [256, 4, 2048], P(('grp', 'seq'), None, 'tp'), may hold values from -6 to 6
- cache_codes: bfloat16 [256, 128, 2048], P(('grp', 'seq'), None, 'tp'), may hold values from -4 to 4
- cache_scales: float32 [256, 8, 16], P(('grp', 'seq'), None, 'tp'), may hold values from 0.5 to 2
- lengths: int32 [256], P(('grp', 'seq')), may hold values from 1 to 128, 16384 in all
- w_out: bfloat16 [8192, 8192], P('tp', 'seq'), may hold values from -0.5 to 0.5
Outputs:
- mixed: bfloat16 [1024, 8192], P(('grp', 'tp'), 'seq')
The draws below stay inside these ranges and needn't reach their ends.
Inputs may be any that keep to these rules, and one draw needn't show every extreme that they name: `block_owner`: the blocks come in aligned groups of 8 consecutive blocks that share one owner and one request; the groups of one prefill device all go to different owners, so a prefill device sends exactly 8 blocks to each owner it sends to. `block_row`: equal on all blocks of one aligned group of 8 blocks.
All inputs are finite; a program needn't handle non-finite values. No bound on the sum of `lengths` on one device may be relied on, other than what follows from the above.
Results may differ from the reference program's by a relative error of at most 0.014.
Values may be sent and summed in bfloat16 or wider, within the bound.
A program may use at most 256 MiB of HBM per device.

```python
import math
import jax
import jax.numpy as jnp
import numpy as np
from jax import lax

D = 8192
HQ = 64
KVH = 8
HD = 128
NEW = 4
BLK = 8
CBLK = 16
ROWS_DEV = 32
CTX = 128
NB_DEV = 64
CAP = 8
PTOK = 4096
NBLK = 512
ROWS = 256
N_GRP = 2
N_SEQ = 4
N_TP = 4


def cache_first(key):
    return jax.random.truncated_normal(jax.random.fold_in(key, 71), -4.0, 4.0, (ROWS, 1, KVH * 2 * HD), jnp.float32)


def group_plan(key):
    senders = NBLK // NB_DEV
    per_sender = NB_DEV // CAP
    sender_keys = jax.random.split(jax.random.fold_in(key, 81), senders)
    picks = jax.vmap(lambda one_key: jax.random.permutation(one_key, senders))(sender_keys)[:, :per_sender]
    owner_of_group = picks.reshape(senders * per_sender).astype(jnp.int32)
    row_of_group = jax.random.randint(jax.random.fold_in(key, 82), (senders * per_sender,), 0, ROWS_DEV).astype(jnp.int32)
    return (jnp.repeat(owner_of_group, CAP), jnp.repeat(row_of_group, CAP))


def draw_block_owner(key, part):
    owner_of_block, row_of_block = group_plan(key)
    return owner_of_block.reshape(NBLK, 1).astype(jnp.int32)


def draw_block_row(key, part):
    owner_of_block, row_of_block = group_plan(key)
    return row_of_block.astype(jnp.int32)


def draw_cache_codes(key, part):
    first_codes = cache_first(key)
    later_codes = jax.random.truncated_normal(jax.random.fold_in(key, 72), -4.0, 4.0, (ROWS, CTX - 1, KVH * 2 * HD), jnp.float32)
    return jnp.concatenate([first_codes, later_codes], axis=1).astype(jnp.bfloat16)


def draw_queries(key, part):
    base_draw = jax.random.truncated_normal(jax.random.fold_in(key, 73), -6.0, 6.0, (ROWS, NEW, HQ * HD), jnp.float32)
    return base_draw.astype(jnp.bfloat16)


def steps_of(stream_key, shape, pieces, least, top_value):
    gain = 1.0
    for dim, shards_of in pieces:
        steps = jax.random.uniform(jax.random.fold_in(jax.random.fold_in(stream_key, 6), dim), (shards_of,), jnp.float32, least / len(pieces), top_value / len(pieces))
        gain = gain * jnp.repeat(jnp.exp(steps), shape[dim] // shards_of).reshape((-1,) + (1,) * (len(shape) - 1 - dim))
    return gain


def split_up(amount, total, most, slope):
    portions = [(1 << 20) // math.isqrt(standing ** slope) + 1 for standing in range(2, amount + 1)]
    spare, holding = total - most - (amount - 1), [1] * (amount - 1)
    while spare > 0:
        free = [i for i in range(amount - 1) if holding[i] < most]
        whole, budget = sum([portions[i] for i in free]), spare
        for i in free:
            more = min(most - holding[i], max(1, budget * portions[i] // whole), spare)
            holding[i] = holding[i] + more
            spare = spare - more
    return np.array([most] + holding)


def uneven(key, amount, total, bound, slope):
    if amount == 2:
        one = jax.random.randint(key, (), max(1, total - bound), min(bound, total - 1) + 1)
        return jnp.stack([one, total - one])
    sizes = jnp.asarray(split_up(amount, total, bound, slope), jnp.int32)
    twos = (amount - 1) // 2
    giver, sink = sizes[1:1 + 2 * twos:2], sizes[2:2 + 2 * twos:2]
    room = jnp.minimum(giver - 1, bound - sink)
    moved = jax.random.randint(jax.random.fold_in(key, 1), (twos,), 0, 1 << 20) % (room + 1)
    sizes = sizes.at[1:1 + 2 * twos:2].set(giver - moved).at[2:2 + 2 * twos:2].set(sink + moved)
    return sizes[jax.random.permutation(jax.random.fold_in(key, 2), amount)]


def gaussian(rng, dims, deviation, reach, shards=(), held_as=jnp.bfloat16):
    drawn = jax.random.normal(rng, dims, jnp.float32) * deviation
    if len(shards) > 0:
        drawn = steps_of(rng, dims, shards, -0.22, 0.18) * drawn
    return jnp.clip(drawn, min=-reach, max=reach).astype(held_as)


def setup_inputs(seed: int = 0) -> dict:
    streams_of = jax.random.split(jax.random.key(seed), 11)
    return {
        "prompt": gaussian(streams_of[0], (PTOK, D), 1.0, 6.0, ((0, 8), (1, 4))),
        "w_kv": gaussian(streams_of[1], (D, KVH * 2 * HD), D ** -0.5, 0.0625, ((1, 4),)),
        "block_owner": draw_block_owner(jax.random.fold_in(streams_of[10], 71), 0),
        "block_row": draw_block_row(jax.random.fold_in(streams_of[10], 71), 0),
        "queries": draw_queries(jax.random.fold_in(streams_of[10], 71), 0),
        "new_kv": gaussian(streams_of[5], (ROWS, NEW, KVH * 2 * HD), 1.0, 6.0, ((0, 8), (2, 4))),
        "cache_codes": draw_cache_codes(jax.random.fold_in(streams_of[10], 71), 0),
        "cache_scales": jnp.clip(jnp.exp(math.log(2.0) - 1.3862944 * jax.random.uniform(streams_of[7], (ROWS, CTX // CBLK, KVH * 2), jnp.float32) ** steps_of(streams_of[7], (ROWS, CTX // CBLK, KVH * 2), ((0, 8), (2, 4)), -0.2, 0.2)), 0.5, 2.0),
        "lengths": uneven(streams_of[8], ROWS, ROWS * CTX // 2, CTX, 2).astype(jnp.int32),
        "w_out": gaussian(streams_of[9], (HQ * HD, D), HD ** -0.5, 0.5, ((0, 4), (1, 4))),
    }


EPS = 1e-05

def rounded(values):
    return lax.optimization_barrier(values.astype(jnp.bfloat16)).astype(jnp.float32)

def reference(prompt, w_kv, block_owner, block_row, queries, new_kv, cache_codes, cache_scales, lengths, w_out):
    widened = prompt.astype(jnp.float32)
    row_scale = lax.rsqrt(lax.optimization_barrier(jnp.sum(widened * widened, axis=1)) / D + EPS)
    prompt_kv = (jnp.dot(prompt, w_kv, preferred_element_type=jnp.float32) * row_scale[:, None]).astype(jnp.bfloat16)
    dest_block = (block_owner[:, 0] * ROWS_DEV + block_row).astype(jnp.int32)
    dest_token = jnp.repeat(dest_block, BLK)
    head_group = HQ // KVH
    query_heads = queries.astype(jnp.float32).reshape(ROWS, NEW, KVH, head_group, HD)
    fresh_all = new_kv.reshape(ROWS, NEW, KVH, 2, HD)
    stored = cache_codes.reshape(ROWS, CTX, KVH, 2, HD)
    block_scales = cache_scales.reshape(ROWS, CTX // CBLK, KVH, 2)
    prompt_heads = prompt_kv.reshape(PTOK, KVH, 2, HD)
    inverse_root = 1.0 / math.sqrt(HD)
    owners = N_GRP * N_SEQ
    zero_index = jnp.zeros((), jnp.int32)

    def attend(pair_index):
        owner_id = pair_index // KVH
        head_id = pair_index % KVH
        first_row = (owner_id * ROWS_DEV).astype(jnp.int32)
        query_part = lax.dynamic_slice(query_heads, (first_row, zero_index, head_id, zero_index, zero_index), (ROWS_DEV, NEW, 1, head_group, HD))[:, :, 0]
        fresh_kv = lax.dynamic_slice(fresh_all, (first_row, zero_index, head_id, zero_index, zero_index), (ROWS_DEV, NEW, 1, 2, HD))[:, :, 0].astype(jnp.float32)
        stored_part = lax.dynamic_slice(stored, (first_row, zero_index, head_id, zero_index, zero_index), (ROWS_DEV, CTX, 1, 2, HD))[:, :, 0].astype(jnp.float32)
        scale_part = lax.dynamic_slice(block_scales, (first_row, zero_index, head_id, zero_index), (ROWS_DEV, CTX // CBLK, 1, 2))[:, :, 0]
        length_part = lax.dynamic_slice(lengths, (first_row,), (ROWS_DEV,))
        prompt_part = lax.dynamic_slice(prompt_heads, (zero_index, head_id, zero_index, zero_index), (PTOK, 1, 2, HD))[:, 0].astype(jnp.float32)
        key_scale = jnp.repeat(scale_part[:, :, 0], CBLK, axis=1)
        value_scale = jnp.repeat(scale_part[:, :, 1], CBLK, axis=1)
        row_ids = first_row + jnp.arange(ROWS_DEV, dtype=jnp.int32)
        s_cache = jnp.einsum('rihd,rpd->rihp', query_part, stored_part[:, :, 0]) * key_scale[:, None, None, :] * inverse_root
        cache_live = jnp.arange(CTX, dtype=jnp.int32)[None, :] < length_part[:, None]
        s_cache = jnp.where(cache_live[:, None, None, :], s_cache, -jnp.inf)
        s_sent = jnp.einsum('rihd,kd->rihk', query_part, prompt_part[:, 0]) * inverse_root
        sent_live = dest_token[None, :] == row_ids[:, None]
        s_sent = jnp.where(sent_live[:, None, None, :], s_sent, -jnp.inf)
        s_fresh = jnp.einsum('rihd,rjd->rihj', query_part, fresh_kv[:, :, 0]) * inverse_root
        causal = jnp.arange(NEW)[None, :] <= jnp.arange(NEW)[:, None]
        s_fresh = jnp.where(causal[None, :, None, :], s_fresh, -jnp.inf)
        row_max = jnp.maximum(jnp.maximum(lax.optimization_barrier(jnp.max(s_cache, axis=-1)), lax.optimization_barrier(jnp.max(s_sent, axis=-1))), lax.optimization_barrier(jnp.max(s_fresh, axis=-1)))
        w_cache = jnp.exp(s_cache - row_max[..., None])
        w_sent = jnp.exp(s_sent - row_max[..., None])
        w_fresh = jnp.exp(s_fresh - row_max[..., None])
        denominator = lax.optimization_barrier(jnp.sum(w_cache, axis=-1)) + lax.optimization_barrier(jnp.sum(w_sent, axis=-1)) + lax.optimization_barrier(jnp.sum(w_fresh, axis=-1))
        numerator = jnp.einsum('rihp,rpd->rihd', rounded(w_cache * value_scale[:, None, None, :]), stored_part[:, :, 1])
        numerator = numerator + jnp.einsum('rihk,kd->rihd', rounded(w_sent), prompt_part[:, 1])
        numerator = numerator + jnp.einsum('rihj,rjd->rihd', rounded(w_fresh), fresh_kv[:, :, 1])
        return (numerator / denominator[..., None]).astype(jnp.bfloat16)
    results = lax.map(attend, jnp.arange(owners * KVH, dtype=jnp.int32))
    results = results.reshape(owners, KVH, ROWS_DEV, NEW, head_group, HD)
    attention = jnp.transpose(results, (0, 2, 3, 1, 4, 5)).reshape(ROWS * NEW, HQ * HD)
    per_group = HQ * HD // N_TP
    mixed = jnp.zeros((ROWS * NEW, D), jnp.float32)
    for group_id in range(N_TP):
        group_term = jnp.dot(attention[:, group_id * per_group:(group_id + 1) * per_group], w_out[group_id * per_group:(group_id + 1) * per_group], preferred_element_type=jnp.float32)
        mixed = mixed + rounded(group_term)
    return mixed.astype(jnp.bfloat16)
```

```python
import functools
import math

import jax
import jax.numpy as jnp
from jax import lax
from jax.experimental import pallas as pl
from jax.experimental.pallas import tpu as pltpu
from jax.sharding import PartitionSpec as P

HQ = 64
KVH = 8
HD = 128
NEW = 4
BLK = 8
CBLK = 16
CAP = 8
GT = BLK * CAP

EPS = 1e-05
MESH = pl.DeviceIdType.MESH
MIB = 1 << 20


def remote(src, dst, send_sem, recv_sem, **where):
    return pltpu.make_async_remote_copy(
        src_ref=src, dst_ref=dst, send_sem=send_sem, recv_sem=recv_sem, device_id=where, device_id_type=MESH
    )


def project_kernel(
    n_grp, n_seq, n_tp,
    match_ref, x_ref, w_ref, ss_ref, rows_ref, pick_ref,
    akv_ref, ameta_ref,
    wbuf, own, pbuf, rbuf, ssbuf, sstot, kvbuf, stage, mstage, kland, mland,
    local_sem, zs, zr, ps, pr, gs, gr, ds, dr, ss_s, ss_r, ks, kr, ms, mr,
):
    me_g, me_s, me_t = lax.axis_index("grp"), lax.axis_index("seq"), lax.axis_index("tp")
    owners = n_grp * n_seq
    me_o = me_g * n_seq + me_s
    features = x_ref.shape[1]
    part = features // owners
    groups = x_ref.shape[0] // GT
    waits = []

    def rows_of(g, s):
        return pl.ds(pl.multiple_of((g * n_seq + s) * part, part), part)

    local = pltpu.make_async_copy(
        w_ref.at[pl.ds(pl.multiple_of(me_t * features, features), features), :], wbuf.at[me_t], local_sem
    )
    local.start()

    barrier = pltpu.get_barrier_semaphore()
    for k in range(1, n_tp):
        pl.semaphore_signal(barrier, inc=1, device_id={"tp": lax.rem(me_t + k, n_tp)}, device_id_type=MESH)
    for j in range(1, owners):
        o = lax.rem(me_o + j, owners)
        pl.semaphore_signal(
            barrier, inc=1, device_id={"grp": o // n_seq, "seq": lax.rem(o, n_seq)}, device_id_type=MESH
        )
    pl.semaphore_wait(barrier, n_tp - 1 + owners - 1)

    for k in range(1, n_tp):
        t = lax.rem(me_t + k, n_tp)
        first = pl.multiple_of(t * features + me_o * part, part)
        copy = remote(
            w_ref.at[pl.ds(first, part), :], wbuf.at[me_t, rows_of(me_g, me_s), :], zs.at[k], zr.at[k], tp=t
        )
        copy.start()
        waits.append(copy)
    for k in range(1, n_tp):
        t = lax.rem(me_t + k, n_tp)
        copy = remote(ss_ref, ssbuf.at[k], ss_s.at[k], ss_r.at[k], tp=t)
        copy.start()
        waits.append(copy)

    local.wait()
    own[...] = jnp.dot(x_ref[...], wbuf[me_t], preferred_element_type=jnp.float32)

    for k in range(1, n_tp):
        t = lax.rem(me_t + n_tp - k, n_tp)
        waits[k - 1].wait_recv()
        mine = wbuf.at[t, rows_of(me_g, me_s), :]
        for j in range(1, n_seq):
            copy = remote(mine, mine, ps.at[k, j], pr.at[k, j], seq=lax.rem(me_s + j, n_seq))
            copy.start()
            waits.append(copy)
        for c in range(1, n_grp):
            copy = remote(mine, mine, gs.at[k, 0, c], gr.at[k, 0, c], grp=lax.rem(me_g + c, n_grp))
            copy.start()
            waits.append(copy)
    sent = []
    for k in range(1, n_tp):
        t = lax.rem(me_t + n_tp - k, n_tp)
        first = len(waits)
        for j in range(1, n_seq):
            s = lax.rem(me_s + n_seq - j, n_seq)
            theirs = wbuf.at[t, rows_of(me_g, s), :]
            remote(theirs, theirs, ps.at[k, j], pr.at[k, j], seq=s).wait_recv()
            for c in range(1, n_grp):
                copy = remote(theirs, theirs, gs.at[k, j, c], gr.at[k, j, c], grp=lax.rem(me_g + c, n_grp))
                copy.start()
                waits.append(copy)
        for j in range(n_seq):
            s = lax.rem(me_s + n_seq - j, n_seq)
            for c in range(1, n_grp):
                g = lax.rem(me_g + n_grp - c, n_grp)
                theirs = wbuf.at[t, rows_of(g, s), :]
                remote(theirs, theirs, gs.at[k, j, c], gr.at[k, j, c], grp=g).wait_recv()
        pbuf[k] = jnp.dot(x_ref[...], wbuf[t], preferred_element_type=jnp.float32).astype(jnp.bfloat16)
        copy = remote(pbuf.at[k], rbuf.at[k], ds.at[k], dr.at[k], tp=t)
        copy.start()
        sent.append(copy)

    total = ss_ref[...]
    for k in range(1, n_tp):
        waits[n_tp - 1 + k - 1].wait_recv()
        total = total + ssbuf[k]
    sstot[...] = total
    for k in range(1, n_tp):
        sent[k - 1].wait_recv()
    acc = own[...]
    for k in range(1, n_tp):
        acc = acc + rbuf[k].astype(jnp.float32)
    kvbuf[...] = acc.astype(jnp.bfloat16)

    out = []
    sub = lax.broadcasted_iota(jnp.int32, (8, 128), 0)
    for j in range(owners):
        o = lax.rem(me_o + j, owners)
        stage[j] = jnp.dot(
            pick_ref[j * GT : (j + 1) * GT], kvbuf[...], preferred_element_type=jnp.float32
        ).astype(jnp.bfloat16)
        sums = match_ref[j, 0] * sstot[0:1, :]
        for i in range(1, groups):
            sums = sums + match_ref[j, i] * sstot[i : i + 1, :]
        mstage[j] = jnp.where(sub == 0, jnp.broadcast_to(sums, (8, 128)), rows_ref[j])
        if j > 0:
            where = dict(grp=o // n_seq, seq=lax.rem(o, n_seq))
            for copy in (
                remote(stage.at[j], kland.at[j], ks.at[j], kr.at[j], **where),
                remote(mstage.at[j], mland.at[j], ms.at[j], mr.at[j], **where),
            ):
                copy.start()
                out.append(copy)
    akv_ref[0] = stage[0]
    ameta_ref[0] = mstage[0]
    for copy in out:
        copy.wait_recv()
    for j in range(1, owners):
        akv_ref[j] = kland[j]
        ameta_ref[j] = mland[j]
    for copy in waits + sent + out:
        copy.wait_send()


def output_kernel(
    n_seq, n_tp, attn_ref, w_ref, out_ref, wv, held, pbuf, rbuf, local_sem, as_, ar, ds, dr
):
    me_s, me_t = lax.axis_index("seq"), lax.axis_index("tp")
    per = n_seq // n_tp
    rows, columns = attn_ref.shape[0], w_ref.shape[1]
    tile = min(512, columns)
    local = pltpu.make_async_copy(w_ref, wv, local_sem)
    local.start()
    barrier = pltpu.get_barrier_semaphore()
    for k in range(1, n_tp):
        pl.semaphore_signal(barrier, inc=1, device_id={"tp": lax.rem(me_t + k, n_tp)}, device_id_type=MESH)
    for j in range(1, n_seq):
        pl.semaphore_signal(barrier, inc=1, device_id={"seq": lax.rem(me_s + j, n_seq)}, device_id_type=MESH)
    pl.semaphore_wait(barrier, n_tp - 1 + n_seq - 1)

    gathers = []
    for j in range(1, n_seq):
        copy = remote(attn_ref, held.at[j], as_.at[j], ar.at[j], seq=lax.rem(me_s + j, n_seq))
        copy.start()
        gathers.append(copy)
    local.wait()
    for j in range(n_seq):
        s = lax.rem(me_s + n_seq - j, n_seq)
        dest, sub = s // per, lax.rem(s, per)
        if j > 0:
            gathers[j - 1].wait_recv()
        block = attn_ref if j == 0 else held.at[j]

        @pl.loop(0, columns // tile)
        def _(c):
            cols = pl.ds(pl.multiple_of(c * tile, tile), tile)
            pbuf[s, :, cols] = jnp.dot(
                block[...], wv[:, cols], preferred_element_type=jnp.float32
            ).astype(jnp.bfloat16)

        @pl.when(dest != me_t)
        def _():
            remote(pbuf.at[s], rbuf.at[me_t, sub], ds.at[s], dr.at[me_t, sub], tp=dest).start()

    acc = [
        pbuf[pl.ds(me_t * per + u, 1)][0].astype(jnp.float32) for u in range(per)
    ]
    for k in range(1, n_tp):
        t = lax.rem(me_t + k, n_tp)
        for u in range(per):
            remote(pbuf.at[0], rbuf.at[t, u], ds.at[0], dr.at[t, u], tp=t).wait_recv()
            acc[u] = acc[u] + rbuf[pl.ds(t, 1), u][0].astype(jnp.float32)
    for u in range(per):
        out_ref[pl.ds(u * rows, rows), :] = acc[u].astype(jnp.bfloat16)
    for copy in gathers:
        copy.wait_send()
    for k in range(1, n_tp):
        t = lax.rem(me_t + k, n_tp)
        for u in range(per):
            s = t * per + u
            remote(pbuf.at[s], rbuf.at[me_t, u], ds.at[s], dr.at[me_t, u], tp=t).wait_send()


def on_device(
    prompt, w_kv, block_owner, block_row, queries, new_kv, cache_codes, cache_scales, lengths, w_out
):
    n_grp, n_seq, n_tp = lax.axis_size("grp"), lax.axis_size("seq"), lax.axis_size("tp")
    owners = n_grp * n_seq
    tokens, features = prompt.shape
    columns = w_kv.shape[1]
    row_count = queries.shape[0]
    groups = tokens // GT

    group_owner = block_owner[:, 0].reshape(groups, CAP)[:, 0]
    group_row = block_row.reshape(groups, CAP)[:, 0]
    me_o = lax.axis_index("grp") * n_seq + lax.axis_index("seq")
    order = (me_o + jnp.arange(owners, dtype=jnp.int32)) % owners
    match = group_owner[None, :] == order[:, None]
    token_of = jnp.arange(owners * GT)[:, None] % GT == jnp.arange(tokens)[None, :] % GT
    pick = jnp.repeat(jnp.repeat(match, GT, axis=0), GT, axis=1) & token_of
    send_row = jnp.sum(jnp.where(match, group_row[None, :] + 1, 0), axis=1) - 1
    row_tiles = jnp.broadcast_to(send_row.astype(jnp.float32)[:, None, None], (owners, 8, 128))
    widened = prompt.astype(jnp.float32)
    squares = jnp.sum(widened * widened, axis=1).reshape(groups, GT)
    squares = jnp.pad(squares, ((0, -groups % 8), (0, 128 - GT)))

    dma = pltpu.SemaphoreType.DMA
    vmem = pl.BlockSpec(memory_space=pltpu.VMEM)
    bf16, f32 = jnp.bfloat16, jnp.float32
    arrived, meta = pl.pallas_call(
        functools.partial(project_kernel, n_grp, n_seq, n_tp),
        out_shape=(
            jax.ShapeDtypeStruct((owners, GT, columns), bf16),
            jax.ShapeDtypeStruct((owners, 8, 128), f32),
        ),
        in_specs=[
            pl.BlockSpec(memory_space=pltpu.SMEM), vmem, pl.BlockSpec(memory_space=pl.ANY), vmem, vmem, vmem,
        ],
        out_specs=(vmem, vmem),
        scratch_shapes=[
            pltpu.VMEM((n_tp, features, columns), bf16),
            pltpu.VMEM((tokens, columns), f32),
            pltpu.VMEM((n_tp, tokens, columns), bf16),
            pltpu.VMEM((n_tp, tokens, columns), bf16),
            pltpu.VMEM((n_tp,) + squares.shape, f32),
            pltpu.VMEM(squares.shape, f32),
            pltpu.VMEM((tokens, columns), bf16),
            pltpu.VMEM((owners, GT, columns), bf16),
            pltpu.VMEM((owners, 8, 128), f32),
            pltpu.VMEM((owners, GT, columns), bf16),
            pltpu.VMEM((owners, 8, 128), f32),
            dma, dma((n_tp,)), dma((n_tp,)),
            dma((n_tp, n_seq)), dma((n_tp, n_seq)),
            dma((n_tp, n_seq, n_grp)), dma((n_tp, n_seq, n_grp)),
            dma((n_tp,)), dma((n_tp,)), dma((n_tp,)), dma((n_tp,)),
            dma((owners,)), dma((owners,)), dma((owners,)), dma((owners,)),
        ],
        compiler_params=pltpu.CompilerParams(
            collective_id=0, has_side_effects=True, vmem_limit_bytes=48 * MIB
        ),
        cost_estimate=pl.CostEstimate(
            flops=2 * tokens * features * columns * n_tp, bytes_accessed=16 * MIB, transcendentals=0
        ),
    )(match.astype(f32), prompt, w_kv, squares, row_tiles, pick.astype(bf16))

    kv_heads = columns // (2 * HD)
    head_group = HQ // KVH
    context = cache_codes.shape[1]
    query_heads = queries.reshape(row_count, NEW, kv_heads, head_group, HD)
    fresh_kv = new_kv.reshape(row_count, NEW, kv_heads, 2, HD)
    stored = cache_codes.reshape(row_count, context, kv_heads, 2, HD)
    block_scales = cache_scales.reshape(row_count, context // CBLK, kv_heads, 2)
    key_scale = jnp.transpose(jnp.repeat(block_scales[:, :, :, 0], CBLK, axis=1), (0, 2, 1))
    value_scale = jnp.transpose(jnp.repeat(block_scales[:, :, :, 1], CBLK, axis=1), (0, 2, 1))
    sent_kv = arrived.reshape(owners * GT, kv_heads, 2, HD)
    sent_rms = lax.rsqrt(meta[:, 0, :GT].reshape(owners * GT) / (features * n_tp) + EPS)
    sent_rows = jnp.repeat(meta[:, 1, 0].astype(jnp.int32), GT)
    inverse_root = 1.0 / math.sqrt(HD)
    row_ids = jnp.arange(row_count, dtype=jnp.int32)
    s_cache = jnp.einsum(
        "rinhd,rpnd->rinhp", query_heads, stored[:, :, :, 0, :], preferred_element_type=jnp.float32
    )
    s_cache = s_cache * key_scale[:, None, :, None, :] * inverse_root
    cache_live = jnp.arange(context, dtype=jnp.int32)[None, :] < lengths[:, None]
    s_cache = jnp.where(cache_live[:, None, None, None, :], s_cache, -jnp.inf)
    s_sent = (
        jnp.einsum(
            "rinhd,knd->rinhk", query_heads, sent_kv[:, :, 0, :], preferred_element_type=jnp.float32
        )
        * sent_rms
        * inverse_root
    )
    sent_live = sent_rows[None, :] == row_ids[:, None]
    s_sent = jnp.where(sent_live[:, None, None, None, :], s_sent, -jnp.inf)
    s_fresh = (
        jnp.einsum(
            "rinhd,rjnd->rinhj",
            query_heads,
            fresh_kv[:, :, :, 0, :],
            preferred_element_type=jnp.float32,
        )
        * inverse_root
    )
    causal = jnp.arange(NEW)[None, :] <= jnp.arange(NEW)[:, None]
    s_fresh = jnp.where(causal[None, :, None, None, :], s_fresh, -jnp.inf)
    row_max = jnp.maximum(
        jnp.maximum(jnp.max(s_cache, axis=-1), jnp.max(s_sent, axis=-1)), jnp.max(s_fresh, axis=-1)
    )
    w_cache = jnp.exp(s_cache - row_max[..., None])
    w_sent = jnp.exp(s_sent - row_max[..., None])
    w_fresh = jnp.exp(s_fresh - row_max[..., None])
    denominator = jnp.sum(w_cache, axis=-1) + jnp.sum(w_sent, axis=-1) + jnp.sum(w_fresh, axis=-1)
    cache_weights = (w_cache * value_scale[:, None, :, None, :]).astype(jnp.bfloat16)
    numerator = jnp.einsum(
        "rinhp,rpnd->rinhd",
        cache_weights,
        stored[:, :, :, 1, :],
        preferred_element_type=jnp.float32,
    )
    numerator = numerator + jnp.einsum(
        "rinhk,knd->rinhd",
        (w_sent * sent_rms).astype(jnp.bfloat16),
        sent_kv[:, :, 1, :],
        preferred_element_type=jnp.float32,
    )
    numerator = numerator + jnp.einsum(
        "rinhj,rjnd->rinhd",
        w_fresh.astype(jnp.bfloat16),
        fresh_kv[:, :, :, 1, :],
        preferred_element_type=jnp.float32,
    )
    attention = (
        (numerator / denominator[..., None])
        .astype(jnp.bfloat16)
        .reshape(row_count * NEW, kv_heads * head_group * HD)
    )
    rows, depth = attention.shape
    per = n_seq // n_tp
    out_columns = w_out.shape[1]
    return pl.pallas_call(
        functools.partial(output_kernel, n_seq, n_tp),
        out_shape=jax.ShapeDtypeStruct((per * rows, out_columns), bf16),
        in_specs=[vmem, pl.BlockSpec(memory_space=pl.ANY)],
        out_specs=vmem,
        scratch_shapes=[
            pltpu.VMEM((depth, out_columns), bf16),
            pltpu.VMEM((n_seq, rows, depth), bf16),
            pltpu.VMEM((n_seq, rows, out_columns), bf16),
            pltpu.VMEM((n_tp, per, rows, out_columns), bf16),
            dma, dma((n_seq,)), dma((n_seq,)), dma((n_seq,)), dma((n_tp, per)),
        ],
        compiler_params=pltpu.CompilerParams(
            collective_id=1, has_side_effects=True, vmem_limit_bytes=48 * MIB
        ),
        cost_estimate=pl.CostEstimate(
            flops=2 * rows * n_seq * depth * out_columns, bytes_accessed=16 * MIB, transcendentals=0
        ),
    )(attention, w_out)


def solution(mesh):
    in_specs = (
        P(("grp", "seq"), "tp"),
        P(None, "tp"),
        P(("grp", "seq"), None),
        P(("grp", "seq")),
        P(("grp", "seq"), None, "tp"),
        P(("grp", "seq"), None, "tp"),
        P(("grp", "seq"), None, "tp"),
        P(("grp", "seq"), None, "tp"),
        P(("grp", "seq")),
        P("tp", "seq"),
    )
    out_specs = P(("grp", "tp"), "seq")
    return jax.shard_map(
        on_device, mesh=mesh, in_specs=in_specs, out_specs=out_specs, check_vma=False
    )
```

```python
import functools
import math

import jax
import jax.numpy as jnp
from jax import lax
from jax.experimental import pallas as pl
from jax.experimental.pallas import tpu as pltpu
from jax.sharding import PartitionSpec as P

HQ = 64
KVH = 8
HD = 128
NEW = 4
BLK = 8
CBLK = 16
CAP = 8
GT = BLK * CAP

EPS = 1e-05
MESH = pl.DeviceIdType.MESH
MIB = 1 << 20


def remote(src, dst, send_sem, recv_sem, **where):
    return pltpu.make_async_remote_copy(
        src_ref=src, dst_ref=dst, send_sem=send_sem, recv_sem=recv_sem, device_id=where, device_id_type=MESH
    )


def project_kernel(
    n_grp, n_seq, n_tp,
    match_ref, x_ref, w_ref, ss_ref, rows_ref, pick_ref,
    akv_ref, ameta_ref,
    wbuf, own, pbuf, rbuf, ssbuf, sstot, kvbuf, stage, mstage, kland, mland,
    local_sem, zs, zr, ps, pr, gs, gr, ds, dr, ss_s, ss_r, ks, kr, ms, mr,
):
    me_g, me_s, me_t = lax.axis_index("grp"), lax.axis_index("seq"), lax.axis_index("tp")
    owners = n_grp * n_seq
    me_o = me_g * n_seq + me_s
    features = x_ref.shape[1]
    part = features // owners
    groups = x_ref.shape[0] // GT
    width = rbuf.shape[-1]
    chunks = w_ref.shape[1] // width
    cols = [slice(c * width, (c + 1) * width) for c in range(chunks)]
    waits = []

    def rows_of(g, s):
        return pl.ds(pl.multiple_of((g * n_seq + s) * part, part), part)

    local = pltpu.make_async_copy(
        w_ref.at[pl.ds(pl.multiple_of(me_t * features, features), features), :], wbuf.at[me_t], local_sem
    )
    local.start()

    barrier = pltpu.get_barrier_semaphore()
    for k in range(1, n_tp):
        pl.semaphore_signal(barrier, inc=1, device_id={"tp": lax.rem(me_t + k, n_tp)}, device_id_type=MESH)
    for j in range(1, owners):
        o = lax.rem(me_o + j, owners)
        pl.semaphore_signal(
            barrier, inc=1, device_id={"grp": o // n_seq, "seq": lax.rem(o, n_seq)}, device_id_type=MESH
        )
    pl.semaphore_wait(barrier, n_tp - 1 + owners - 1)

    def w_sends(c):
        copies = []
        for k in range(1, n_tp):
            t = lax.rem(me_t + k, n_tp)
            first = pl.multiple_of(t * features + me_o * part, part)
            copies.append(remote(
                w_ref.at[pl.ds(first, part), cols[c]], wbuf.at[me_t, rows_of(me_g, me_s), cols[c]],
                zs.at[c, k], zr.at[c, k], tp=t,
            ))
            copies[-1].start()
        return copies

    w_copies = [w_sends(0)]
    ss_copies = []
    for k in range(1, n_tp):
        copy = remote(ss_ref, ssbuf.at[k], ss_s.at[k], ss_r.at[k], tp=lax.rem(me_t + k, n_tp))
        copy.start()
        ss_copies.append(copy)

    local.wait()
    own[...] = jnp.dot(x_ref[...], wbuf[me_t], preferred_element_type=jnp.float32)
    for c in range(1, chunks):
        for copy in w_copies[c - 1]:
            copy.wait_send()
        w_copies.append(w_sends(c))
    for copy in w_copies[-1]:
        waits.append(copy)
    waits.extend(ss_copies)

    for c in range(chunks):
        for k in range(1, n_tp):
            t = lax.rem(me_t + n_tp - k, n_tp)
            w_copies[c][k - 1].wait_recv()
            mine = wbuf.at[t, rows_of(me_g, me_s), cols[c]]
            for j in range(1, n_seq):
                copy = remote(mine, mine, ps.at[c, k, j], pr.at[c, k, j], seq=lax.rem(me_s + j, n_seq))
                copy.start()
                waits.append(copy)
            for e in range(1, n_grp):
                copy = remote(mine, mine, gs.at[c, k, 0, e], gr.at[c, k, 0, e], grp=lax.rem(me_g + e, n_grp))
                copy.start()
                waits.append(copy)
    sent = []
    for c in range(chunks):
        for k in range(1, n_tp):
            t = lax.rem(me_t + n_tp - k, n_tp)
            for j in range(1, n_seq):
                s = lax.rem(me_s + n_seq - j, n_seq)
                theirs = wbuf.at[t, rows_of(me_g, s), cols[c]]
                remote(theirs, theirs, ps.at[c, k, j], pr.at[c, k, j], seq=s).wait_recv()
                for e in range(1, n_grp):
                    copy = remote(
                        theirs, theirs, gs.at[c, k, j, e], gr.at[c, k, j, e], grp=lax.rem(me_g + e, n_grp)
                    )
                    copy.start()
                    waits.append(copy)
        for k in range(1, n_tp):
            t = lax.rem(me_t + n_tp - k, n_tp)
            for j in range(n_seq):
                s = lax.rem(me_s + n_seq - j, n_seq)
                for e in range(1, n_grp):
                    g = lax.rem(me_g + n_grp - e, n_grp)
                    theirs = wbuf.at[t, rows_of(g, s), cols[c]]
                    remote(theirs, theirs, gs.at[c, k, j, e], gr.at[c, k, j, e], grp=g).wait_recv()
            pbuf[k, c] = jnp.dot(
                x_ref[...], wbuf[t, :, cols[c]], preferred_element_type=jnp.float32
            ).astype(jnp.bfloat16)
            copy = remote(pbuf.at[k, c], rbuf.at[k, c], ds.at[c, k], dr.at[c, k], tp=t)
            copy.start()
            sent.append(copy)

    total = ss_ref[...]
    for k in range(1, n_tp):
        ss_copies[k - 1].wait_recv()
        total = total + ssbuf[k]
    sstot[...] = total
    for c in range(chunks):
        acc = own[:, cols[c]]
        for k in range(1, n_tp):
            sent[c * (n_tp - 1) + k - 1].wait_recv()
            acc = acc + rbuf[k, c].astype(jnp.float32)
        kvbuf[:, cols[c]] = acc.astype(jnp.bfloat16)

    out = []
    sub = lax.broadcasted_iota(jnp.int32, (8, 128), 0)
    for j in range(owners):
        o = lax.rem(me_o + j, owners)
        stage[j] = jnp.dot(
            pick_ref[j * GT : (j + 1) * GT], kvbuf[...], preferred_element_type=jnp.float32
        ).astype(jnp.bfloat16)
        sums = match_ref[j, 0] * sstot[0:1, :]
        for i in range(1, groups):
            sums = sums + match_ref[j, i] * sstot[i : i + 1, :]
        mstage[j] = jnp.where(sub == 0, jnp.broadcast_to(sums, (8, 128)), rows_ref[j])
        if j > 0:
            where = dict(grp=o // n_seq, seq=lax.rem(o, n_seq))
            for copy in (
                remote(stage.at[j], kland.at[j], ks.at[j], kr.at[j], **where),
                remote(mstage.at[j], mland.at[j], ms.at[j], mr.at[j], **where),
            ):
                copy.start()
                out.append(copy)
    akv_ref[0] = stage[0]
    ameta_ref[0] = mstage[0]
    for copy in out:
        copy.wait_recv()
    for j in range(1, owners):
        akv_ref[j] = kland[j]
        ameta_ref[j] = mland[j]
    for copy in waits + sent + out:
        copy.wait_send()


def attention_kernel(
    kv_heads, head_group, inverse_root,
    lengths_ref, q_ref, new_ref, cache_ref, scale_ref, sent_ref, rms_ref, rows_ref, out_ref,
):
    f32, bf16 = jnp.float32, jnp.bfloat16
    step_rows, context = cache_ref.shape[0], cache_ref.shape[1]
    head_rows = head_group * NEW
    all_rows = step_rows * head_rows
    first = pl.program_id(0) * step_rows
    position = lax.broadcasted_iota(jnp.int32, (head_rows, context), 1)

    def scores(a, b):
        return lax.dot_general(a, b, (((1,), (1,)), ((), ())), preferred_element_type=f32)

    sent_count, new_count = sent_ref.shape[0], step_rows * NEW
    of_row = lax.broadcasted_iota(jnp.int32, (all_rows, sent_count), 0) // head_rows + first
    sent_live = rows_ref[...] == of_row.astype(f32)
    row = lax.broadcasted_iota(jnp.int32, (all_rows, new_count), 0)
    column = lax.broadcasted_iota(jnp.int32, (all_rows, new_count), 1)
    new_live = (column // NEW == row // head_rows) & (column % NEW <= row % NEW)
    for n in range(kv_heads):
        key = slice(n * 2 * HD, n * 2 * HD + HD)
        value = slice(n * 2 * HD + HD, (n + 1) * 2 * HD)
        q = q_ref[n]
        parts = []
        for r in range(step_rows):
            part = scores(q[r * head_rows : (r + 1) * head_rows], cache_ref[r, :, key])
            part = part * scale_ref[n, 0, r : r + 1, :] * inverse_root
            parts.append(jnp.where(position < lengths_ref[first + r], part, -jnp.inf))
        s_cache = jnp.concatenate(parts, axis=0)
        s_sent = scores(q, sent_ref[:, key]) * rms_ref[...] * inverse_root
        s_sent = jnp.where(sent_live, s_sent, -jnp.inf)
        s_new = jnp.where(new_live, scores(q, new_ref[:, key]) * inverse_root, -jnp.inf)
        top = jnp.maximum(
            jnp.maximum(jnp.max(s_cache, axis=1, keepdims=True), jnp.max(s_sent, axis=1, keepdims=True)),
            jnp.max(s_new, axis=1, keepdims=True),
        )
        w_cache, w_sent, w_new = jnp.exp(s_cache - top), jnp.exp(s_sent - top), jnp.exp(s_new - top)
        denominator = (
            jnp.sum(w_cache, axis=1, keepdims=True)
            + jnp.sum(w_sent, axis=1, keepdims=True)
            + jnp.sum(w_new, axis=1, keepdims=True)
        )
        parts = []
        for r in range(step_rows):
            part = w_cache[r * head_rows : (r + 1) * head_rows] * scale_ref[n, 1, r : r + 1, :]
            parts.append(jnp.dot(part.astype(bf16), cache_ref[r, :, value], preferred_element_type=f32))
        total = jnp.concatenate(parts, axis=0)
        total = total + jnp.dot(
            (w_sent * rms_ref[...]).astype(bf16), sent_ref[:, value], preferred_element_type=f32
        )
        total = total + jnp.dot(w_new.astype(bf16), new_ref[:, value], preferred_element_type=f32)
        out_ref[n] = (total / denominator).astype(bf16)


def output_kernel(
    n_seq, n_tp, attn_ref, w_ref, out_ref, wv, held, pbuf, rbuf, local_sem, as_, ar, ds, dr
):
    me_s, me_t = lax.axis_index("seq"), lax.axis_index("tp")
    per = n_seq // n_tp
    rows, columns = attn_ref.shape[0], w_ref.shape[1]
    tile = min(512, columns)
    local = pltpu.make_async_copy(w_ref, wv, local_sem)
    local.start()
    barrier = pltpu.get_barrier_semaphore()
    for k in range(1, n_tp):
        pl.semaphore_signal(barrier, inc=1, device_id={"tp": lax.rem(me_t + k, n_tp)}, device_id_type=MESH)
    for j in range(1, n_seq):
        pl.semaphore_signal(barrier, inc=1, device_id={"seq": lax.rem(me_s + j, n_seq)}, device_id_type=MESH)
    pl.semaphore_wait(barrier, n_tp - 1 + n_seq - 1)

    gathers = []
    for j in range(1, n_seq):
        copy = remote(attn_ref, held.at[j], as_.at[j], ar.at[j], seq=lax.rem(me_s + j, n_seq))
        copy.start()
        gathers.append(copy)
    local.wait()
    for j in range(n_seq):
        s = lax.rem(me_s + n_seq - j, n_seq)
        dest, sub = s // per, lax.rem(s, per)
        if j > 0:
            gathers[j - 1].wait_recv()
        block = attn_ref if j == 0 else held.at[j]

        @pl.loop(0, columns // tile)
        def _(c):
            cols = pl.ds(pl.multiple_of(c * tile, tile), tile)
            pbuf[s, :, cols] = jnp.dot(
                block[...], wv[:, cols], preferred_element_type=jnp.float32
            ).astype(jnp.bfloat16)

        @pl.when(dest != me_t)
        def _():
            remote(pbuf.at[s], rbuf.at[me_t, sub], ds.at[s], dr.at[me_t, sub], tp=dest).start()

    acc = [
        pbuf[pl.ds(me_t * per + u, 1)][0].astype(jnp.float32) for u in range(per)
    ]
    for k in range(1, n_tp):
        t = lax.rem(me_t + k, n_tp)
        for u in range(per):
            remote(pbuf.at[0], rbuf.at[t, u], ds.at[0], dr.at[t, u], tp=t).wait_recv()
            acc[u] = acc[u] + rbuf[pl.ds(t, 1), u][0].astype(jnp.float32)
    for u in range(per):
        out_ref[pl.ds(u * rows, rows), :] = acc[u].astype(jnp.bfloat16)
    for copy in gathers:
        copy.wait_send()
    for k in range(1, n_tp):
        t = lax.rem(me_t + k, n_tp)
        for u in range(per):
            s = t * per + u
            remote(pbuf.at[s], rbuf.at[me_t, u], ds.at[s], dr.at[me_t, u], tp=t).wait_send()


def on_device(
    prompt, w_kv, block_owner, block_row, queries, new_kv, cache_codes, cache_scales, lengths, w_out
):
    n_grp, n_seq, n_tp = lax.axis_size("grp"), lax.axis_size("seq"), lax.axis_size("tp")
    owners = n_grp * n_seq
    tokens, features = prompt.shape
    columns = w_kv.shape[1]
    row_count = queries.shape[0]
    groups = tokens // GT

    group_owner = block_owner[:, 0].reshape(groups, CAP)[:, 0]
    group_row = block_row.reshape(groups, CAP)[:, 0]
    me_o = lax.axis_index("grp") * n_seq + lax.axis_index("seq")
    order = (me_o + jnp.arange(owners, dtype=jnp.int32)) % owners
    match = group_owner[None, :] == order[:, None]
    token_of = jnp.arange(owners * GT)[:, None] % GT == jnp.arange(tokens)[None, :] % GT
    pick = jnp.repeat(jnp.repeat(match, GT, axis=0), GT, axis=1) & token_of
    send_row = jnp.sum(jnp.where(match, group_row[None, :] + 1, 0), axis=1) - 1
    row_tiles = jnp.broadcast_to(send_row.astype(jnp.float32)[:, None, None], (owners, 8, 128))
    widened = prompt.astype(jnp.float32)
    squares = jnp.sum(widened * widened, axis=1).reshape(groups, GT)
    squares = jnp.pad(squares, ((0, -groups % 8), (0, 128 - GT)))

    width = min(256, columns)
    chunks = columns // width
    dma = pltpu.SemaphoreType.DMA
    vmem = pl.BlockSpec(memory_space=pltpu.VMEM)
    bf16, f32 = jnp.bfloat16, jnp.float32
    arrived, meta = pl.pallas_call(
        functools.partial(project_kernel, n_grp, n_seq, n_tp),
        out_shape=(
            jax.ShapeDtypeStruct((owners, GT, columns), bf16),
            jax.ShapeDtypeStruct((owners, 8, 128), f32),
        ),
        in_specs=[
            pl.BlockSpec(memory_space=pltpu.SMEM), vmem, pl.BlockSpec(memory_space=pl.ANY), vmem, vmem, vmem,
        ],
        out_specs=(vmem, vmem),
        scratch_shapes=[
            pltpu.VMEM((n_tp, features, columns), bf16),
            pltpu.VMEM((tokens, columns), f32),
            pltpu.VMEM((n_tp, chunks, tokens, width), bf16),
            pltpu.VMEM((n_tp, chunks, tokens, width), bf16),
            pltpu.VMEM((n_tp,) + squares.shape, f32),
            pltpu.VMEM(squares.shape, f32),
            pltpu.VMEM((tokens, columns), bf16),
            pltpu.VMEM((owners, GT, columns), bf16),
            pltpu.VMEM((owners, 8, 128), f32),
            pltpu.VMEM((owners, GT, columns), bf16),
            pltpu.VMEM((owners, 8, 128), f32),
            dma, dma((chunks, n_tp)), dma((chunks, n_tp)),
            dma((chunks, n_tp, n_seq)), dma((chunks, n_tp, n_seq)),
            dma((chunks, n_tp, n_seq, n_grp)), dma((chunks, n_tp, n_seq, n_grp)),
            dma((chunks, n_tp)), dma((chunks, n_tp)), dma((n_tp,)), dma((n_tp,)),
            dma((owners,)), dma((owners,)), dma((owners,)), dma((owners,)),
        ],
        compiler_params=pltpu.CompilerParams(
            collective_id=0, has_side_effects=True, vmem_limit_bytes=48 * MIB
        ),
        cost_estimate=pl.CostEstimate(
            flops=2 * tokens * features * columns * n_tp, bytes_accessed=16 * MIB, transcendentals=0
        ),
    )(match.astype(f32), prompt, w_kv, squares, row_tiles, pick.astype(bf16))

    kv_heads = columns // (2 * HD)
    head_group = HQ // KVH
    context = cache_codes.shape[1]
    inverse_root = 1.0 / math.sqrt(HD)
    head_rows = head_group * NEW
    query_heads = jnp.transpose(
        queries.reshape(row_count, NEW, kv_heads, head_group, HD), (2, 0, 3, 1, 4)
    ).reshape(kv_heads, row_count * head_rows, HD)
    block_scales = jnp.transpose(
        cache_scales.reshape(row_count, context // CBLK, kv_heads, 2), (2, 3, 0, 1)
    )
    scales = jnp.repeat(block_scales, CBLK, axis=3)
    sent_rms = lax.rsqrt(meta[:, 0, :GT].reshape(1, owners * GT) / (features * n_tp) + EPS)
    sent_rows = jnp.repeat(meta[:, 1, 0], GT)[None, :]
    step_rows = 8
    attention = pl.pallas_call(
        functools.partial(attention_kernel, kv_heads, head_group, inverse_root),
        grid=(row_count // step_rows,),
        out_shape=jax.ShapeDtypeStruct((kv_heads, row_count * head_rows, HD), bf16),
        in_specs=[
            pl.BlockSpec(memory_space=pltpu.SMEM),
            pl.BlockSpec((kv_heads, step_rows * head_rows, HD), lambda i: (0, i, 0)),
            pl.BlockSpec((step_rows * NEW, columns), lambda i: (i, 0)),
            pl.BlockSpec((step_rows, context, columns), lambda i: (i, 0, 0)),
            pl.BlockSpec((kv_heads, 2, step_rows, context), lambda i: (0, 0, i, 0)),
            pl.BlockSpec((owners * GT, columns), lambda i: (0, 0)),
            pl.BlockSpec((1, owners * GT), lambda i: (0, 0)),
            pl.BlockSpec((1, owners * GT), lambda i: (0, 0)),
        ],
        out_specs=pl.BlockSpec((kv_heads, step_rows * head_rows, HD), lambda i: (0, i, 0)),
        compiler_params=pltpu.CompilerParams(vmem_limit_bytes=32 * MIB),
        cost_estimate=pl.CostEstimate(
            flops=4 * row_count * head_rows * kv_heads * HD * (context + owners * GT),
            bytes_accessed=8 * MIB, transcendentals=0,
        ),
    )(
        lengths, query_heads, new_kv.reshape(row_count * NEW, columns), cache_codes, scales,
        arrived.reshape(owners * GT, columns), sent_rms, sent_rows,
    )
    attention = jnp.transpose(
        attention.reshape(kv_heads, row_count, head_group, NEW, HD), (1, 3, 0, 2, 4)
    ).reshape(row_count * NEW, kv_heads * head_group * HD)
    rows, depth = attention.shape
    per = n_seq // n_tp
    out_columns = w_out.shape[1]
    return pl.pallas_call(
        functools.partial(output_kernel, n_seq, n_tp),
        out_shape=jax.ShapeDtypeStruct((per * rows, out_columns), bf16),
        in_specs=[vmem, pl.BlockSpec(memory_space=pl.ANY)],
        out_specs=vmem,
        scratch_shapes=[
            pltpu.VMEM((depth, out_columns), bf16),
            pltpu.VMEM((n_seq, rows, depth), bf16),
            pltpu.VMEM((n_seq, rows, out_columns), bf16),
            pltpu.VMEM((n_tp, per, rows, out_columns), bf16),
            dma, dma((n_seq,)), dma((n_seq,)), dma((n_seq,)), dma((n_tp, per)),
        ],
        compiler_params=pltpu.CompilerParams(
            collective_id=1, has_side_effects=True, vmem_limit_bytes=48 * MIB
        ),
        cost_estimate=pl.CostEstimate(
            flops=2 * rows * n_seq * depth * out_columns, bytes_accessed=16 * MIB, transcendentals=0
        ),
    )(attention, w_out)


def solution(mesh):
    in_specs = (
        P(("grp", "seq"), "tp"),
        P(None, "tp"),
        P(("grp", "seq"), None),
        P(("grp", "seq")),
        P(("grp", "seq"), None, "tp"),
        P(("grp", "seq"), None, "tp"),
        P(("grp", "seq"), None, "tp"),
        P(("grp", "seq"), None, "tp"),
        P(("grp", "seq")),
        P("tp", "seq"),
    )
    out_specs = P(("grp", "tp"), "seq")
    return jax.shard_map(
        on_device, mesh=mesh, in_specs=in_specs, out_specs=out_specs, check_vma=False
    )
```

```python
import functools
import math

import jax
import jax.numpy as jnp
from jax import lax
from jax.experimental import pallas as pl
from jax.experimental.pallas import tpu as pltpu
from jax.sharding import PartitionSpec as P

HQ = 64
KVH = 8
HD = 128
NEW = 4
BLK = 8
CBLK = 16
CAP = 8
GT = BLK * CAP

EPS = 1e-05
MESH = pl.DeviceIdType.MESH
MIB = 1 << 20


def remote(src, dst, send_sem, recv_sem, **where):
    return pltpu.make_async_remote_copy(
        src_ref=src, dst_ref=dst, send_sem=send_sem, recv_sem=recv_sem, device_id=where, device_id_type=MESH
    )


def pass_on(z, n, d, acc, mine, landing, send_sem, recv_sem):
    for way, step in ((0, 1), (1, -1)):
        @pl.when((d - z) * step > 0)
        def _():
            begins = z == (0 if step > 0 else n - 1)

            @pl.when(jnp.logical_not(begins))
            def _():
                remote(mine, landing.at[way], send_sem, recv_sem.at[way], tp=z - step).wait_recv()
                mine[...] = (acc[...] + landing[way].astype(jnp.float32)).astype(jnp.bfloat16)

            @pl.when(begins)
            def _():
                mine[...] = acc[...].astype(jnp.bfloat16)

            remote(mine, landing.at[way], send_sem, recv_sem.at[way], tp=z + step).start()


def take_in(z, n, acc, landing, recv_sem):
    for way, begins in ((0, 0), (1, n - 1)):
        @pl.when(z != begins)
        def _():
            other = z - 1 if way == 0 else z + 1
            remote(landing.at[way], landing.at[way], recv_sem.at[way], recv_sem.at[way], tp=other).wait_recv()
            acc[...] += landing[way].astype(jnp.float32)


def project_kernel(
    n_grp, n_seq, n_tp,
    match_ref, x_ref, w_ref, ss_ref, rows_ref, pick_ref,
    akv_ref, ameta_ref,
    wbuf, own, acc, pbuf, rbuf, ssbuf, sstot, kvbuf, stage, mstage, kland, mland,
    local_sem, zs, zr, ps, pr, gs, gr, ds, dr, ss_s, ss_r, ks, kr, ms, mr,
):
    me_g, me_s, me_t = lax.axis_index("grp"), lax.axis_index("seq"), lax.axis_index("tp")
    owners = n_grp * n_seq
    me_o = me_g * n_seq + me_s
    features = x_ref.shape[1]
    part = features // owners
    groups = x_ref.shape[0] // GT
    width = rbuf.shape[-1]
    chunks = w_ref.shape[1] // width
    cols = [slice(c * width, (c + 1) * width) for c in range(chunks)]
    waits = []

    def rows_of(g, s):
        return pl.ds(pl.multiple_of((g * n_seq + s) * part, part), part)

    local = pltpu.make_async_copy(
        w_ref.at[pl.ds(pl.multiple_of(me_t * features, features), features), :], wbuf.at[me_t], local_sem
    )
    local.start()

    barrier = pltpu.get_barrier_semaphore()
    for k in range(1, n_tp):
        pl.semaphore_signal(barrier, inc=1, device_id={"tp": lax.rem(me_t + k, n_tp)}, device_id_type=MESH)
    for j in range(1, owners):
        o = lax.rem(me_o + j, owners)
        pl.semaphore_signal(
            barrier, inc=1, device_id={"grp": o // n_seq, "seq": lax.rem(o, n_seq)}, device_id_type=MESH
        )
    pl.semaphore_wait(barrier, n_tp - 1 + owners - 1)

    def w_sends(c):
        copies = []
        for k in range(1, n_tp):
            t = lax.rem(me_t + k, n_tp)
            first = pl.multiple_of(t * features + me_o * part, part)
            copies.append(remote(
                w_ref.at[pl.ds(first, part), cols[c]], wbuf.at[me_t, rows_of(me_g, me_s), cols[c]],
                zs.at[c, k], zr.at[c, k], tp=t,
            ))
            copies[-1].start()
        return copies

    w_copies = [w_sends(0)]
    ss_copies = []
    for k in range(1, n_tp):
        copy = remote(ss_ref, ssbuf.at[k], ss_s.at[k], ss_r.at[k], tp=lax.rem(me_t + k, n_tp))
        copy.start()
        ss_copies.append(copy)

    local.wait()
    own[...] = jnp.dot(x_ref[...], wbuf[me_t], preferred_element_type=jnp.float32)
    for c in range(1, chunks):
        for copy in w_copies[c - 1]:
            copy.wait_send()
        w_copies.append(w_sends(c))
    for copy in w_copies[-1]:
        waits.append(copy)
    waits.extend(ss_copies)

    for c in range(chunks):
        for k in range(1, n_tp):
            t = lax.rem(me_t + n_tp - k, n_tp)
            w_copies[c][k - 1].wait_recv()
            mine = wbuf.at[t, rows_of(me_g, me_s), cols[c]]
            for j in range(1, n_seq):
                copy = remote(mine, mine, ps.at[c, k, j], pr.at[c, k, j], seq=lax.rem(me_s + j, n_seq))
                copy.start()
                waits.append(copy)
            for e in range(1, n_grp):
                copy = remote(mine, mine, gs.at[c, k, 0, e], gr.at[c, k, 0, e], grp=lax.rem(me_g + e, n_grp))
                copy.start()
                waits.append(copy)
    dest_order = sorted(range(n_tp), key=lambda d: (min(d, n_tp - 1 - d), -d))
    for c in range(chunks):
        for k in range(1, n_tp):
            t = lax.rem(me_t + n_tp - k, n_tp)
            for j in range(1, n_seq):
                s = lax.rem(me_s + n_seq - j, n_seq)
                theirs = wbuf.at[t, rows_of(me_g, s), cols[c]]
                remote(theirs, theirs, ps.at[c, k, j], pr.at[c, k, j], seq=s).wait_recv()
                for e in range(1, n_grp):
                    copy = remote(
                        theirs, theirs, gs.at[c, k, j, e], gr.at[c, k, j, e], grp=lax.rem(me_g + e, n_grp)
                    )
                    copy.start()
                    waits.append(copy)
        for d in dest_order:
            k = lax.rem(me_t + n_tp - d, n_tp)

            @pl.when(me_t != d)
            def _():
                for j in range(n_seq):
                    s = lax.rem(me_s + n_seq - j, n_seq)
                    for e in range(1, n_grp):
                        g = lax.rem(me_g + n_grp - e, n_grp)
                        theirs = wbuf.at[d, rows_of(g, s), cols[c]]
                        remote(theirs, theirs, gs.at[c, k, j, e], gr.at[c, k, j, e], grp=g).wait_recv()
                acc[...] = jnp.dot(x_ref[...], wbuf[d, :, cols[c]], preferred_element_type=jnp.float32)
                pass_on(me_t, n_tp, d, acc, pbuf.at[d, c], rbuf.at[:, d, c], ds.at[c, d], dr.at[:, c, d])

    total = ss_ref[...]
    for k in range(1, n_tp):
        ss_copies[k - 1].wait_recv()
        total = total + ssbuf[k]
    sstot[...] = total
    for c in range(chunks):
        acc[...] = own[:, cols[c]]
        take_in(me_t, n_tp, acc, rbuf.at[:, me_t, c], dr.at[:, c, me_t])
        kvbuf[:, cols[c]] = acc[...].astype(jnp.bfloat16)

    out = []
    sub = lax.broadcasted_iota(jnp.int32, (8, 128), 0)
    for j in range(owners):
        o = lax.rem(me_o + j, owners)
        stage[j] = jnp.dot(
            pick_ref[j * GT : (j + 1) * GT], kvbuf[...], preferred_element_type=jnp.float32
        ).astype(jnp.bfloat16)
        sums = match_ref[j, 0] * sstot[0:1, :]
        for i in range(1, groups):
            sums = sums + match_ref[j, i] * sstot[i : i + 1, :]
        mstage[j] = jnp.where(sub == 0, jnp.broadcast_to(sums, (8, 128)), rows_ref[j])
        if j > 0:
            where = dict(grp=o // n_seq, seq=lax.rem(o, n_seq))
            for copy in (
                remote(stage.at[j], kland.at[j], ks.at[j], kr.at[j], **where),
                remote(mstage.at[j], mland.at[j], ms.at[j], mr.at[j], **where),
            ):
                copy.start()
                out.append(copy)
    akv_ref[0] = stage[0]
    ameta_ref[0] = mstage[0]
    for copy in out:
        copy.wait_recv()
    for j in range(1, owners):
        akv_ref[j] = kland[j]
        ameta_ref[j] = mland[j]
    for copy in waits + out:
        copy.wait_send()
    for c in range(chunks):
        for d in range(n_tp):
            @pl.when(me_t != d)
            def _():
                remote(pbuf.at[d, c], rbuf.at[0, d, c], ds.at[c, d], dr.at[0, c, d], tp=d).wait_send()


def attention_kernel(
    kv_heads, head_group, inverse_root,
    lengths_ref, q_ref, new_ref, cache_ref, scale_ref, sent_ref, rms_ref, rows_ref, out_ref,
):
    f32, bf16 = jnp.float32, jnp.bfloat16
    step_rows, context = cache_ref.shape[0], cache_ref.shape[1]
    head_rows = head_group * NEW
    all_rows = step_rows * head_rows
    first = pl.program_id(0) * step_rows
    position = lax.broadcasted_iota(jnp.int32, (head_rows, context), 1)

    def scores(a, b):
        return lax.dot_general(a, b, (((1,), (1,)), ((), ())), preferred_element_type=f32)

    sent_count, new_count = sent_ref.shape[0], step_rows * NEW
    of_row = lax.broadcasted_iota(jnp.int32, (all_rows, sent_count), 0) // head_rows + first
    sent_live = rows_ref[...] == of_row.astype(f32)
    row = lax.broadcasted_iota(jnp.int32, (all_rows, new_count), 0)
    column = lax.broadcasted_iota(jnp.int32, (all_rows, new_count), 1)
    new_live = (column // NEW == row // head_rows) & (column % NEW <= row % NEW)
    for n in range(kv_heads):
        key = slice(n * 2 * HD, n * 2 * HD + HD)
        value = slice(n * 2 * HD + HD, (n + 1) * 2 * HD)
        q = q_ref[n]
        parts = []
        for r in range(step_rows):
            part = scores(q[r * head_rows : (r + 1) * head_rows], cache_ref[r, :, key])
            part = part * scale_ref[n, 0, r : r + 1, :] * inverse_root
            parts.append(jnp.where(position < lengths_ref[first + r], part, -jnp.inf))
        s_cache = jnp.concatenate(parts, axis=0)
        s_sent = scores(q, sent_ref[:, key]) * rms_ref[...] * inverse_root
        s_sent = jnp.where(sent_live, s_sent, -jnp.inf)
        s_new = jnp.where(new_live, scores(q, new_ref[:, key]) * inverse_root, -jnp.inf)
        top = jnp.maximum(
            jnp.maximum(jnp.max(s_cache, axis=1, keepdims=True), jnp.max(s_sent, axis=1, keepdims=True)),
            jnp.max(s_new, axis=1, keepdims=True),
        )
        w_cache, w_sent, w_new = jnp.exp(s_cache - top), jnp.exp(s_sent - top), jnp.exp(s_new - top)
        denominator = (
            jnp.sum(w_cache, axis=1, keepdims=True)
            + jnp.sum(w_sent, axis=1, keepdims=True)
            + jnp.sum(w_new, axis=1, keepdims=True)
        )
        parts = []
        for r in range(step_rows):
            part = w_cache[r * head_rows : (r + 1) * head_rows] * scale_ref[n, 1, r : r + 1, :]
            parts.append(jnp.dot(part.astype(bf16), cache_ref[r, :, value], preferred_element_type=f32))
        total = jnp.concatenate(parts, axis=0)
        total = total + jnp.dot(
            (w_sent * rms_ref[...]).astype(bf16), sent_ref[:, value], preferred_element_type=f32
        )
        total = total + jnp.dot(w_new.astype(bf16), new_ref[:, value], preferred_element_type=f32)
        out_ref[n] = (total / denominator).astype(bf16)


def output_kernel(
    n_seq, n_tp, attn_ref, w_ref, out_ref, wv, held, acc, own, pbuf, rbuf, local_sem, as_, ar, ds, dr
):
    me_s, me_t = lax.axis_index("seq"), lax.axis_index("tp")
    per = n_seq // n_tp
    rows, columns = attn_ref.shape[0], w_ref.shape[1]
    tile = acc.shape[1]
    local = pltpu.make_async_copy(w_ref, wv, local_sem)
    local.start()
    barrier = pltpu.get_barrier_semaphore()
    for k in range(1, n_tp):
        pl.semaphore_signal(barrier, inc=1, device_id={"tp": lax.rem(me_t + k, n_tp)}, device_id_type=MESH)
    for j in range(1, n_seq):
        pl.semaphore_signal(barrier, inc=1, device_id={"seq": lax.rem(me_s + j, n_seq)}, device_id_type=MESH)
    pl.semaphore_wait(barrier, n_tp - 1 + n_seq - 1)

    gathers = []
    for j in range(1, n_seq):
        copy = remote(attn_ref, held.at[j], as_.at[j], ar.at[j], seq=lax.rem(me_s + j, n_seq))
        copy.start()
        gathers.append(copy)
    local.wait()
    for j in range(n_seq):
        s = lax.rem(me_s + n_seq - j, n_seq)
        dest, sub = s // per, lax.rem(s, per)
        if j > 0:
            gathers[j - 1].wait_recv()
        block = attn_ref if j == 0 else held.at[j]

        @pl.loop(0, columns // tile)
        def _(c):
            acc[...] = jnp.dot(
                block[...], wv[:, pl.ds(pl.multiple_of(c * tile, tile), tile)], preferred_element_type=jnp.float32
            )

            @pl.when(dest == me_t)
            def _():
                own[sub, c] = acc[...]

            @pl.when(dest != me_t)
            def _():
                pass_on(me_t, n_tp, dest, acc, pbuf.at[s, c], rbuf.at[:, s, c], ds.at[s, c], dr.at[:, s, c])

    for u in range(per):
        for c in range(columns // tile):
            s = me_t * per + u
            acc[...] = own[u, c]
            take_in(me_t, n_tp, acc, rbuf.at[:, s, c], dr.at[:, s, c])
            out_ref[u * rows : (u + 1) * rows, c * tile : (c + 1) * tile] = acc[...].astype(jnp.bfloat16)
    for copy in gathers:
        copy.wait_send()
    for k in range(1, n_tp):
        t = lax.rem(me_t + k, n_tp)
        for u in range(per):
            s = t * per + u
            for c in range(columns // tile):
                remote(pbuf.at[s, c], rbuf.at[0, s, c], ds.at[s, c], dr.at[0, s, c], tp=t).wait_send()


def on_device(
    prompt, w_kv, block_owner, block_row, queries, new_kv, cache_codes, cache_scales, lengths, w_out
):
    n_grp, n_seq, n_tp = lax.axis_size("grp"), lax.axis_size("seq"), lax.axis_size("tp")
    owners = n_grp * n_seq
    tokens, features = prompt.shape
    columns = w_kv.shape[1]
    row_count = queries.shape[0]
    groups = tokens // GT

    group_owner = block_owner[:, 0].reshape(groups, CAP)[:, 0]
    group_row = block_row.reshape(groups, CAP)[:, 0]
    me_o = lax.axis_index("grp") * n_seq + lax.axis_index("seq")
    order = (me_o + jnp.arange(owners, dtype=jnp.int32)) % owners
    match = group_owner[None, :] == order[:, None]
    token_of = jnp.arange(owners * GT)[:, None] % GT == jnp.arange(tokens)[None, :] % GT
    pick = jnp.repeat(jnp.repeat(match, GT, axis=0), GT, axis=1) & token_of
    send_row = jnp.sum(jnp.where(match, group_row[None, :] + 1, 0), axis=1) - 1
    row_tiles = jnp.broadcast_to(send_row.astype(jnp.float32)[:, None, None], (owners, 8, 128))
    widened = prompt.astype(jnp.float32)
    squares = jnp.sum(widened * widened, axis=1).reshape(groups, GT)
    squares = jnp.pad(squares, ((0, -groups % 8), (0, 128 - GT)))

    width = min(256, columns)
    chunks = columns // width
    dma = pltpu.SemaphoreType.DMA
    vmem = pl.BlockSpec(memory_space=pltpu.VMEM)
    bf16, f32 = jnp.bfloat16, jnp.float32
    arrived, meta = pl.pallas_call(
        functools.partial(project_kernel, n_grp, n_seq, n_tp),
        out_shape=(
            jax.ShapeDtypeStruct((owners, GT, columns), bf16),
            jax.ShapeDtypeStruct((owners, 8, 128), f32),
        ),
        in_specs=[
            pl.BlockSpec(memory_space=pltpu.SMEM), vmem, pl.BlockSpec(memory_space=pl.ANY), vmem, vmem, vmem,
        ],
        out_specs=(vmem, vmem),
        scratch_shapes=[
            pltpu.VMEM((n_tp, features, columns), bf16),
            pltpu.VMEM((tokens, columns), f32),
            pltpu.VMEM((tokens, width), f32),
            pltpu.VMEM((n_tp, chunks, tokens, width), bf16),
            pltpu.VMEM((2, n_tp, chunks, tokens, width), bf16),
            pltpu.VMEM((n_tp,) + squares.shape, f32),
            pltpu.VMEM(squares.shape, f32),
            pltpu.VMEM((tokens, columns), bf16),
            pltpu.VMEM((owners, GT, columns), bf16),
            pltpu.VMEM((owners, 8, 128), f32),
            pltpu.VMEM((owners, GT, columns), bf16),
            pltpu.VMEM((owners, 8, 128), f32),
            dma, dma((chunks, n_tp)), dma((chunks, n_tp)),
            dma((chunks, n_tp, n_seq)), dma((chunks, n_tp, n_seq)),
            dma((chunks, n_tp, n_seq, n_grp)), dma((chunks, n_tp, n_seq, n_grp)),
            dma((chunks, n_tp)), dma((2, chunks, n_tp)), dma((n_tp,)), dma((n_tp,)),
            dma((owners,)), dma((owners,)), dma((owners,)), dma((owners,)),
        ],
        compiler_params=pltpu.CompilerParams(
            collective_id=0, has_side_effects=True, vmem_limit_bytes=48 * MIB
        ),
        cost_estimate=pl.CostEstimate(
            flops=2 * tokens * features * columns * n_tp, bytes_accessed=16 * MIB, transcendentals=0
        ),
    )(match.astype(f32), prompt, w_kv, squares, row_tiles, pick.astype(bf16))

    kv_heads = columns // (2 * HD)
    head_group = HQ // KVH
    context = cache_codes.shape[1]
    inverse_root = 1.0 / math.sqrt(HD)
    head_rows = head_group * NEW
    query_heads = jnp.transpose(
        queries.reshape(row_count, NEW, kv_heads, head_group, HD), (2, 0, 3, 1, 4)
    ).reshape(kv_heads, row_count * head_rows, HD)
    block_scales = jnp.transpose(
        cache_scales.reshape(row_count, context // CBLK, kv_heads, 2), (2, 3, 0, 1)
    )
    scales = jnp.repeat(block_scales, CBLK, axis=3)
    sent_rms = lax.rsqrt(meta[:, 0, :GT].reshape(1, owners * GT) / (features * n_tp) + EPS)
    sent_rows = jnp.repeat(meta[:, 1, 0], GT)[None, :]
    step_rows = 8
    attention = pl.pallas_call(
        functools.partial(attention_kernel, kv_heads, head_group, inverse_root),
        grid=(row_count // step_rows,),
        out_shape=jax.ShapeDtypeStruct((kv_heads, row_count * head_rows, HD), bf16),
        in_specs=[
            pl.BlockSpec(memory_space=pltpu.SMEM),
            pl.BlockSpec((kv_heads, step_rows * head_rows, HD), lambda i: (0, i, 0)),
            pl.BlockSpec((step_rows * NEW, columns), lambda i: (i, 0)),
            pl.BlockSpec((step_rows, context, columns), lambda i: (i, 0, 0)),
            pl.BlockSpec((kv_heads, 2, step_rows, context), lambda i: (0, 0, i, 0)),
            pl.BlockSpec((owners * GT, columns), lambda i: (0, 0)),
            pl.BlockSpec((1, owners * GT), lambda i: (0, 0)),
            pl.BlockSpec((1, owners * GT), lambda i: (0, 0)),
        ],
        out_specs=pl.BlockSpec((kv_heads, step_rows * head_rows, HD), lambda i: (0, i, 0)),
        compiler_params=pltpu.CompilerParams(vmem_limit_bytes=32 * MIB),
        cost_estimate=pl.CostEstimate(
            flops=4 * row_count * head_rows * kv_heads * HD * (context + owners * GT),
            bytes_accessed=8 * MIB, transcendentals=0,
        ),
    )(
        lengths, query_heads, new_kv.reshape(row_count * NEW, columns), cache_codes, scales,
        arrived.reshape(owners * GT, columns), sent_rms, sent_rows,
    )
    attention = jnp.transpose(
        attention.reshape(kv_heads, row_count, head_group, NEW, HD), (1, 3, 0, 2, 4)
    ).reshape(row_count * NEW, kv_heads * head_group * HD)
    rows, depth = attention.shape
    per = n_seq // n_tp
    out_columns = w_out.shape[1]
    tile = min(512, out_columns)
    tiles = out_columns // tile
    return pl.pallas_call(
        functools.partial(output_kernel, n_seq, n_tp),
        out_shape=jax.ShapeDtypeStruct((per * rows, out_columns), bf16),
        in_specs=[vmem, pl.BlockSpec(memory_space=pl.ANY)],
        out_specs=vmem,
        scratch_shapes=[
            pltpu.VMEM((depth, out_columns), bf16),
            pltpu.VMEM((n_seq, rows, depth), bf16),
            pltpu.VMEM((rows, tile), f32),
            pltpu.VMEM((per, tiles, rows, tile), f32),
            pltpu.VMEM((n_seq, tiles, rows, tile), bf16),
            pltpu.VMEM((2, n_seq, tiles, rows, tile), bf16),
            dma, dma((n_seq,)), dma((n_seq,)), dma((n_seq, tiles)), dma((2, n_seq, tiles)),
        ],
        compiler_params=pltpu.CompilerParams(
            collective_id=1, has_side_effects=True, vmem_limit_bytes=48 * MIB
        ),
        cost_estimate=pl.CostEstimate(
            flops=2 * rows * n_seq * depth * out_columns, bytes_accessed=16 * MIB, transcendentals=0
        ),
    )(attention, w_out)


def solution(mesh):
    in_specs = (
        P(("grp", "seq"), "tp"),
        P(None, "tp"),
        P(("grp", "seq"), None),
        P(("grp", "seq")),
        P(("grp", "seq"), None, "tp"),
        P(("grp", "seq"), None, "tp"),
        P(("grp", "seq"), None, "tp"),
        P(("grp", "seq"), None, "tp"),
        P(("grp", "seq")),
        P("tp", "seq"),
    )
    out_specs = P(("grp", "tp"), "seq")
    return jax.shard_map(
        on_device, mesh=mesh, in_specs=in_specs, out_specs=out_specs, check_vma=False
    )
```

```python
import functools
import math

import jax
import jax.numpy as jnp
from jax import lax
from jax.experimental import pallas as pl
from jax.experimental.pallas import tpu as pltpu
from jax.sharding import PartitionSpec as P

HQ = 64
KVH = 8
HD = 128
NEW = 4
BLK = 8
CBLK = 16
CAP = 8
GT = BLK * CAP

EPS = 1e-05
MESH = pl.DeviceIdType.MESH
MIB = 1 << 20


def remote(src, dst, send_sem, recv_sem, **where):
    return pltpu.make_async_remote_copy(
        src_ref=src, dst_ref=dst, send_sem=send_sem, recv_sem=recv_sem, device_id=where, device_id_type=MESH
    )


def pass_on(z, n, d, acc, mine, landing, send_sem, recv_sem):
    for way, step in ((0, 1), (1, -1)):
        @pl.when((d - z) * step > 0)
        def _():
            begins = z == (0 if step > 0 else n - 1)

            @pl.when(jnp.logical_not(begins))
            def _():
                remote(mine, landing.at[way], send_sem, recv_sem.at[way], tp=z - step).wait_recv()
                mine[...] = (acc[...] + landing[way].astype(jnp.float32)).astype(jnp.bfloat16)

            @pl.when(begins)
            def _():
                mine[...] = acc[...].astype(jnp.bfloat16)

            remote(mine, landing.at[way], send_sem, recv_sem.at[way], tp=z + step).start()


def take_in(z, n, acc, landing, recv_sem):
    for way, begins in ((0, 0), (1, n - 1)):
        @pl.when(z != begins)
        def _():
            other = z - 1 if way == 0 else z + 1
            remote(landing.at[way], landing.at[way], recv_sem.at[way], recv_sem.at[way], tp=other).wait_recv()
            acc[...] += landing[way].astype(jnp.float32)


def project_kernel(
    n_grp, n_seq, n_tp,
    match_ref, x_ref, w_ref, ss_ref, rows_ref, pick_ref,
    akv_ref, ameta_ref,
    wbuf, own, acc, pbuf, rbuf, ssbuf, sstot, kvbuf, stage, mstage, kland, mland,
    local_sem, zs, zr, ps, pr, gs, gr, ds, dr, ss_s, ss_r, ks, kr, ms, mr,
):
    me_g, me_s, me_t = lax.axis_index("grp"), lax.axis_index("seq"), lax.axis_index("tp")
    owners = n_grp * n_seq
    me_o = me_g * n_seq + me_s
    features = x_ref.shape[1]
    part = features // owners
    groups = x_ref.shape[0] // GT
    width = rbuf.shape[-1]
    chunks = w_ref.shape[1] // width
    cols = [slice(c * width, (c + 1) * width) for c in range(chunks)]
    half = x_ref.shape[0] // 2
    halves = [slice(0, half), slice(half, 2 * half)]
    waits = []

    def rows_of(g, s):
        return pl.ds(pl.multiple_of((g * n_seq + s) * part, part), part)

    local = pltpu.make_async_copy(
        w_ref.at[pl.ds(pl.multiple_of(me_t * features, features), features), :], wbuf.at[me_t], local_sem
    )
    local.start()

    barrier = pltpu.get_barrier_semaphore()
    for k in range(1, n_tp):
        pl.semaphore_signal(barrier, inc=1, device_id={"tp": lax.rem(me_t + k, n_tp)}, device_id_type=MESH)
    for j in range(1, owners):
        o = lax.rem(me_o + j, owners)
        pl.semaphore_signal(
            barrier, inc=1, device_id={"grp": o // n_seq, "seq": lax.rem(o, n_seq)}, device_id_type=MESH
        )
    pl.semaphore_wait(barrier, n_tp - 1 + owners - 1)

    def w_sends(c):
        copies = []
        for k in range(1, n_tp):
            t = lax.rem(me_t + k, n_tp)
            first = pl.multiple_of(t * features + me_o * part, part)
            copies.append(remote(
                w_ref.at[pl.ds(first, part), cols[c]], wbuf.at[me_t, rows_of(me_g, me_s), cols[c]],
                zs.at[c, k], zr.at[c, k], tp=t,
            ))
            copies[-1].start()
        return copies

    w_copies = [w_sends(0)]
    ss_copies = []
    for k in range(1, n_tp):
        copy = remote(ss_ref, ssbuf.at[k], ss_s.at[k], ss_r.at[k], tp=lax.rem(me_t + k, n_tp))
        copy.start()
        ss_copies.append(copy)

    local.wait()
    own[...] = jnp.dot(x_ref[...], wbuf[me_t], preferred_element_type=jnp.float32)
    for c in range(1, chunks):
        for copy in w_copies[c - 1]:
            copy.wait_send()
        w_copies.append(w_sends(c))
    for copy in w_copies[-1]:
        waits.append(copy)
    waits.extend(ss_copies)

    for c in range(chunks):
        for k in range(1, n_tp):
            t = lax.rem(me_t + n_tp - k, n_tp)
            w_copies[c][k - 1].wait_recv()
            mine = wbuf.at[t, rows_of(me_g, me_s), cols[c]]
            for j in range(1, n_seq):
                copy = remote(mine, mine, ps.at[c, k, j], pr.at[c, k, j], seq=lax.rem(me_s + j, n_seq))
                copy.start()
                waits.append(copy)
            for e in range(1, n_grp):
                copy = remote(mine, mine, gs.at[c, k, 0, e], gr.at[c, k, 0, e], grp=lax.rem(me_g + e, n_grp))
                copy.start()
                waits.append(copy)
    dest_order = sorted(range(n_tp), key=lambda d: (min(d, n_tp - 1 - d), -d))
    for c in range(chunks):
        for k in range(1, n_tp):
            t = lax.rem(me_t + n_tp - k, n_tp)
            for j in range(1, n_seq):
                s = lax.rem(me_s + n_seq - j, n_seq)
                theirs = wbuf.at[t, rows_of(me_g, s), cols[c]]
                remote(theirs, theirs, ps.at[c, k, j], pr.at[c, k, j], seq=s).wait_recv()
                for e in range(1, n_grp):
                    copy = remote(
                        theirs, theirs, gs.at[c, k, j, e], gr.at[c, k, j, e], grp=lax.rem(me_g + e, n_grp)
                    )
                    copy.start()
                    waits.append(copy)
        for d in dest_order:
            k = lax.rem(me_t + n_tp - d, n_tp)

            @pl.when(me_t != d)
            def _():
                for j in range(n_seq):
                    s = lax.rem(me_s + n_seq - j, n_seq)
                    for e in range(1, n_grp):
                        g = lax.rem(me_g + n_grp - e, n_grp)
                        theirs = wbuf.at[d, rows_of(g, s), cols[c]]
                        remote(theirs, theirs, gs.at[c, k, j, e], gr.at[c, k, j, e], grp=g).wait_recv()
                for h, rows in enumerate(halves):
                    acc[rows] = jnp.dot(x_ref[rows], wbuf[d, :, cols[c]], preferred_element_type=jnp.float32)
                    pass_on(
                        me_t, n_tp, d, acc.at[rows], pbuf.at[d, c, rows], rbuf.at[:, d, c, rows],
                        ds.at[c, d, h], dr.at[:, c, d, h],
                    )

    total = ss_ref[...]
    for k in range(1, n_tp):
        ss_copies[k - 1].wait_recv()
        total = total + ssbuf[k]
    sstot[...] = total
    for c in range(chunks):
        acc[...] = own[:, cols[c]]
        for h, rows in enumerate(halves):
            take_in(me_t, n_tp, acc.at[rows], rbuf.at[:, me_t, c, rows], dr.at[:, c, me_t, h])
        kvbuf[:, cols[c]] = acc[...].astype(jnp.bfloat16)

    out = []
    sub = lax.broadcasted_iota(jnp.int32, (8, 128), 0)
    for j in range(owners):
        o = lax.rem(me_o + j, owners)
        stage[j] = jnp.dot(
            pick_ref[j * GT : (j + 1) * GT], kvbuf[...], preferred_element_type=jnp.float32
        ).astype(jnp.bfloat16)
        sums = match_ref[j, 0] * sstot[0:1, :]
        for i in range(1, groups):
            sums = sums + match_ref[j, i] * sstot[i : i + 1, :]
        mstage[j] = jnp.where(sub == 0, jnp.broadcast_to(sums, (8, 128)), rows_ref[j])
        if j > 0:
            where = dict(grp=o // n_seq, seq=lax.rem(o, n_seq))
            for copy in (
                remote(stage.at[j], kland.at[j], ks.at[j], kr.at[j], **where),
                remote(mstage.at[j], mland.at[j], ms.at[j], mr.at[j], **where),
            ):
                copy.start()
                out.append(copy)
    akv_ref[0] = stage[0]
    ameta_ref[0] = mstage[0]
    for copy in out:
        copy.wait_recv()
    for j in range(1, owners):
        akv_ref[j] = kland[j]
        ameta_ref[j] = mland[j]
    for copy in waits + out:
        copy.wait_send()
    for c in range(chunks):
        for d in range(n_tp):
            @pl.when(me_t != d)
            def _():
                for h, rows in enumerate(halves):
                    remote(
                        pbuf.at[d, c, rows], rbuf.at[0, d, c, rows], ds.at[c, d, h], dr.at[0, c, d, h], tp=d
                    ).wait_send()


def attention_kernel(
    kv_heads, head_group, inverse_root,
    lengths_ref, q_ref, new_ref, cache_ref, scale_ref, sent_ref, rms_ref, rows_ref, out_ref,
):
    f32, bf16 = jnp.float32, jnp.bfloat16
    step_rows, context = cache_ref.shape[0], cache_ref.shape[1]
    head_rows = head_group * NEW
    all_rows = step_rows * head_rows
    first = pl.program_id(0) * step_rows
    position = lax.broadcasted_iota(jnp.int32, (head_rows, context), 1)

    def scores(a, b):
        return lax.dot_general(a, b, (((1,), (1,)), ((), ())), preferred_element_type=f32)

    sent_count, new_count = sent_ref.shape[0], step_rows * NEW
    of_row = lax.broadcasted_iota(jnp.int32, (all_rows, sent_count), 0) // head_rows + first
    sent_live = rows_ref[...] == of_row.astype(f32)
    row = lax.broadcasted_iota(jnp.int32, (all_rows, new_count), 0)
    column = lax.broadcasted_iota(jnp.int32, (all_rows, new_count), 1)
    new_live = (column // NEW == row // head_rows) & (column % NEW <= row % NEW)
    for n in range(kv_heads):
        key = slice(n * 2 * HD, n * 2 * HD + HD)
        value = slice(n * 2 * HD + HD, (n + 1) * 2 * HD)
        q = q_ref[n]
        parts = []
        for r in range(step_rows):
            part = scores(q[r * head_rows : (r + 1) * head_rows], cache_ref[r, :, key])
            part = part * scale_ref[n, 0, r : r + 1, :] * inverse_root
            parts.append(jnp.where(position < lengths_ref[first + r], part, -jnp.inf))
        s_cache = jnp.concatenate(parts, axis=0)
        s_sent = scores(q, sent_ref[:, key]) * rms_ref[...] * inverse_root
        s_sent = jnp.where(sent_live, s_sent, -jnp.inf)
        s_new = jnp.where(new_live, scores(q, new_ref[:, key]) * inverse_root, -jnp.inf)
        top = jnp.maximum(
            jnp.maximum(jnp.max(s_cache, axis=1, keepdims=True), jnp.max(s_sent, axis=1, keepdims=True)),
            jnp.max(s_new, axis=1, keepdims=True),
        )
        w_cache, w_sent, w_new = jnp.exp(s_cache - top), jnp.exp(s_sent - top), jnp.exp(s_new - top)
        denominator = (
            jnp.sum(w_cache, axis=1, keepdims=True)
            + jnp.sum(w_sent, axis=1, keepdims=True)
            + jnp.sum(w_new, axis=1, keepdims=True)
        )
        parts = []
        for r in range(step_rows):
            part = w_cache[r * head_rows : (r + 1) * head_rows] * scale_ref[n, 1, r : r + 1, :]
            parts.append(jnp.dot(part.astype(bf16), cache_ref[r, :, value], preferred_element_type=f32))
        total = jnp.concatenate(parts, axis=0)
        total = total + jnp.dot(
            (w_sent * rms_ref[...]).astype(bf16), sent_ref[:, value], preferred_element_type=f32
        )
        total = total + jnp.dot(w_new.astype(bf16), new_ref[:, value], preferred_element_type=f32)
        out_ref[n] = (total / denominator).astype(bf16)


def output_kernel(
    n_seq, n_tp, attn_ref, w_ref, out_ref, wv, held, acc, own, pbuf, rbuf, local_sem, as_, ar, ds, dr
):
    me_s, me_t = lax.axis_index("seq"), lax.axis_index("tp")
    per = n_seq // n_tp
    rows, columns = attn_ref.shape[0], w_ref.shape[1]
    tile = acc.shape[1]
    local = pltpu.make_async_copy(w_ref, wv, local_sem)
    local.start()
    barrier = pltpu.get_barrier_semaphore()
    for k in range(1, n_tp):
        pl.semaphore_signal(barrier, inc=1, device_id={"tp": lax.rem(me_t + k, n_tp)}, device_id_type=MESH)
    for j in range(1, n_seq):
        pl.semaphore_signal(barrier, inc=1, device_id={"seq": lax.rem(me_s + j, n_seq)}, device_id_type=MESH)
    pl.semaphore_wait(barrier, n_tp - 1 + n_seq - 1)

    gathers = []

    def gather(src, dst, i, s):
        copy = remote(src, dst, as_.at[i], ar.at[i], seq=s)
        copy.start()
        gathers.append(copy)

    square = n_seq == 4
    if square:
        beside, above = me_s + 1 - 2 * lax.rem(me_s, 2), lax.rem(me_s + 2, 4)
        sources = [me_s, beside, above, lax.rem(beside + 2, 4)]
        half = rows // 2
        gather(attn_ref, held.at[1], 1, beside)
        gather(attn_ref, held.at[2], 2, above)
    else:
        sources = [lax.rem(me_s + n_seq - j, n_seq) for j in range(n_seq)]
        for j in range(1, n_seq):
            gather(attn_ref, held.at[j], j, lax.rem(me_s + j, n_seq))
    local.wait()
    for j in range(n_seq):
        s = sources[j]
        dest, sub = s // per, lax.rem(s, per)
        if square and j == 1:
            gathers[0].wait_recv()
            gather(held.at[1, :half], held.at[3, :half], 3, above)
            gathers[1].wait_recv()
            gather(held.at[2, half:], held.at[3, half:], 4, beside)
        elif square and j == 3:
            gathers[2].wait_recv()
            gathers[3].wait_recv()
        elif j > 0 and not square:
            gathers[j - 1].wait_recv()
        block = attn_ref if j == 0 else held.at[j]

        @pl.loop(0, columns // tile)
        def _(c):
            acc[...] = jnp.dot(
                block[...], wv[:, pl.ds(pl.multiple_of(c * tile, tile), tile)], preferred_element_type=jnp.float32
            )

            @pl.when(dest == me_t)
            def _():
                own[sub, c] = acc[...]

            @pl.when(dest != me_t)
            def _():
                pass_on(me_t, n_tp, dest, acc, pbuf.at[s, c], rbuf.at[:, s, c], ds.at[s, c], dr.at[:, s, c])

    for u in range(per):
        for c in range(columns // tile):
            s = me_t * per + u
            acc[...] = own[u, c]
            take_in(me_t, n_tp, acc, rbuf.at[:, s, c], dr.at[:, s, c])
            out_ref[u * rows : (u + 1) * rows, c * tile : (c + 1) * tile] = acc[...].astype(jnp.bfloat16)
    for copy in gathers:
        copy.wait_send()
    for k in range(1, n_tp):
        t = lax.rem(me_t + k, n_tp)
        for u in range(per):
            s = t * per + u
            for c in range(columns // tile):
                remote(pbuf.at[s, c], rbuf.at[0, s, c], ds.at[s, c], dr.at[0, s, c], tp=t).wait_send()


def on_device(
    prompt, w_kv, block_owner, block_row, queries, new_kv, cache_codes, cache_scales, lengths, w_out
):
    n_grp, n_seq, n_tp = lax.axis_size("grp"), lax.axis_size("seq"), lax.axis_size("tp")
    owners = n_grp * n_seq
    tokens, features = prompt.shape
    columns = w_kv.shape[1]
    row_count = queries.shape[0]
    groups = tokens // GT

    group_owner = block_owner[:, 0].reshape(groups, CAP)[:, 0]
    group_row = block_row.reshape(groups, CAP)[:, 0]
    me_o = lax.axis_index("grp") * n_seq + lax.axis_index("seq")
    order = (me_o + jnp.arange(owners, dtype=jnp.int32)) % owners
    match = group_owner[None, :] == order[:, None]
    token_of = jnp.arange(owners * GT)[:, None] % GT == jnp.arange(tokens)[None, :] % GT
    pick = jnp.repeat(jnp.repeat(match, GT, axis=0), GT, axis=1) & token_of
    send_row = jnp.sum(jnp.where(match, group_row[None, :] + 1, 0), axis=1) - 1
    row_tiles = jnp.broadcast_to(send_row.astype(jnp.float32)[:, None, None], (owners, 8, 128))
    widened = prompt.astype(jnp.float32)
    squares = jnp.sum(widened * widened, axis=1).reshape(groups, GT)
    squares = jnp.pad(squares, ((0, -groups % 8), (0, 128 - GT)))

    width = min(256, columns)
    chunks = columns // width
    dma = pltpu.SemaphoreType.DMA
    vmem = pl.BlockSpec(memory_space=pltpu.VMEM)
    bf16, f32 = jnp.bfloat16, jnp.float32
    arrived, meta = pl.pallas_call(
        functools.partial(project_kernel, n_grp, n_seq, n_tp),
        out_shape=(
            jax.ShapeDtypeStruct((owners, GT, columns), bf16),
            jax.ShapeDtypeStruct((owners, 8, 128), f32),
        ),
        in_specs=[
            pl.BlockSpec(memory_space=pltpu.SMEM), vmem, pl.BlockSpec(memory_space=pl.ANY), vmem, vmem, vmem,
        ],
        out_specs=(vmem, vmem),
        scratch_shapes=[
            pltpu.VMEM((n_tp, features, columns), bf16),
            pltpu.VMEM((tokens, columns), f32),
            pltpu.VMEM((tokens, width), f32),
            pltpu.VMEM((n_tp, chunks, tokens, width), bf16),
            pltpu.VMEM((2, n_tp, chunks, tokens, width), bf16),
            pltpu.VMEM((n_tp,) + squares.shape, f32),
            pltpu.VMEM(squares.shape, f32),
            pltpu.VMEM((tokens, columns), bf16),
            pltpu.VMEM((owners, GT, columns), bf16),
            pltpu.VMEM((owners, 8, 128), f32),
            pltpu.VMEM((owners, GT, columns), bf16),
            pltpu.VMEM((owners, 8, 128), f32),
            dma, dma((chunks, n_tp)), dma((chunks, n_tp)),
            dma((chunks, n_tp, n_seq)), dma((chunks, n_tp, n_seq)),
            dma((chunks, n_tp, n_seq, n_grp)), dma((chunks, n_tp, n_seq, n_grp)),
            dma((chunks, n_tp, 2)), dma((2, chunks, n_tp, 2)), dma((n_tp,)), dma((n_tp,)),
            dma((owners,)), dma((owners,)), dma((owners,)), dma((owners,)),
        ],
        compiler_params=pltpu.CompilerParams(
            collective_id=0, has_side_effects=True, vmem_limit_bytes=48 * MIB
        ),
        cost_estimate=pl.CostEstimate(
            flops=2 * tokens * features * columns * n_tp, bytes_accessed=16 * MIB, transcendentals=0
        ),
    )(match.astype(f32), prompt, w_kv, squares, row_tiles, pick.astype(bf16))

    kv_heads = columns // (2 * HD)
    head_group = HQ // KVH
    context = cache_codes.shape[1]
    inverse_root = 1.0 / math.sqrt(HD)
    head_rows = head_group * NEW
    query_heads = jnp.transpose(
        queries.reshape(row_count, NEW, kv_heads, head_group, HD), (2, 0, 3, 1, 4)
    ).reshape(kv_heads, row_count * head_rows, HD)
    block_scales = jnp.transpose(
        cache_scales.reshape(row_count, context // CBLK, kv_heads, 2), (2, 3, 0, 1)
    )
    scales = jnp.repeat(block_scales, CBLK, axis=3)
    sent_rms = lax.rsqrt(meta[:, 0, :GT].reshape(1, owners * GT) / (features * n_tp) + EPS)
    sent_rows = jnp.repeat(meta[:, 1, 0], GT)[None, :]
    step_rows = 8
    attention = pl.pallas_call(
        functools.partial(attention_kernel, kv_heads, head_group, inverse_root),
        grid=(row_count // step_rows,),
        out_shape=jax.ShapeDtypeStruct((kv_heads, row_count * head_rows, HD), bf16),
        in_specs=[
            pl.BlockSpec(memory_space=pltpu.SMEM),
            pl.BlockSpec((kv_heads, step_rows * head_rows, HD), lambda i: (0, i, 0)),
            pl.BlockSpec((step_rows * NEW, columns), lambda i: (i, 0)),
            pl.BlockSpec((step_rows, context, columns), lambda i: (i, 0, 0)),
            pl.BlockSpec((kv_heads, 2, step_rows, context), lambda i: (0, 0, i, 0)),
            pl.BlockSpec((owners * GT, columns), lambda i: (0, 0)),
            pl.BlockSpec((1, owners * GT), lambda i: (0, 0)),
            pl.BlockSpec((1, owners * GT), lambda i: (0, 0)),
        ],
        out_specs=pl.BlockSpec((kv_heads, step_rows * head_rows, HD), lambda i: (0, i, 0)),
        compiler_params=pltpu.CompilerParams(vmem_limit_bytes=32 * MIB),
        cost_estimate=pl.CostEstimate(
            flops=4 * row_count * head_rows * kv_heads * HD * (context + owners * GT),
            bytes_accessed=8 * MIB, transcendentals=0,
        ),
    )(
        lengths, query_heads, new_kv.reshape(row_count * NEW, columns), cache_codes, scales,
        arrived.reshape(owners * GT, columns), sent_rms, sent_rows,
    )
    attention = jnp.transpose(
        attention.reshape(kv_heads, row_count, head_group, NEW, HD), (1, 3, 0, 2, 4)
    ).reshape(row_count * NEW, kv_heads * head_group * HD)
    rows, depth = attention.shape
    per = n_seq // n_tp
    out_columns = w_out.shape[1]
    tile = min(512, out_columns)
    tiles = out_columns // tile
    return pl.pallas_call(
        functools.partial(output_kernel, n_seq, n_tp),
        out_shape=jax.ShapeDtypeStruct((per * rows, out_columns), bf16),
        in_specs=[vmem, pl.BlockSpec(memory_space=pl.ANY)],
        out_specs=vmem,
        scratch_shapes=[
            pltpu.VMEM((depth, out_columns), bf16),
            pltpu.VMEM((n_seq, rows, depth), bf16),
            pltpu.VMEM((rows, tile), f32),
            pltpu.VMEM((per, tiles, rows, tile), f32),
            pltpu.VMEM((n_seq, tiles, rows, tile), bf16),
            pltpu.VMEM((2, n_seq, tiles, rows, tile), bf16),
            dma, dma((n_seq + 1,)), dma((n_seq + 1,)), dma((n_seq, tiles)), dma((2, n_seq, tiles)),
        ],
        compiler_params=pltpu.CompilerParams(
            collective_id=1, has_side_effects=True, vmem_limit_bytes=48 * MIB
        ),
        cost_estimate=pl.CostEstimate(
            flops=2 * rows * n_seq * depth * out_columns, bytes_accessed=16 * MIB, transcendentals=0
        ),
    )(attention, w_out)


def solution(mesh):
    in_specs = (
        P(("grp", "seq"), "tp"),
        P(None, "tp"),
        P(("grp", "seq"), None),
        P(("grp", "seq")),
        P(("grp", "seq"), None, "tp"),
        P(("grp", "seq"), None, "tp"),
        P(("grp", "seq"), None, "tp"),
        P(("grp", "seq"), None, "tp"),
        P(("grp", "seq")),
        P("tp", "seq"),
    )
    out_specs = P(("grp", "tp"), "seq")
    return jax.shard_map(
        on_device, mesh=mesh, in_specs=in_specs, out_specs=out_specs, check_vma=False
    )
```

```python
import functools
import math

import jax
import jax.numpy as jnp
from jax import lax
from jax.experimental import pallas as pl
from jax.experimental.pallas import tpu as pltpu
from jax.sharding import PartitionSpec as P

HQ = 64
KVH = 8
HD = 128
NEW = 4
BLK = 8
CBLK = 16
CAP = 8
GT = BLK * CAP

EPS = 1e-05
MESH = pl.DeviceIdType.MESH
MIB = 1 << 20


def remote(src, dst, send_sem, recv_sem, **where):
    return pltpu.make_async_remote_copy(
        src_ref=src, dst_ref=dst, send_sem=send_sem, recv_sem=recv_sem, device_id=where, device_id_type=MESH
    )


def pass_on(z, n, d, acc, mine, landing, send_sem, recv_sem):
    for way, step in ((0, 1), (1, -1)):
        @pl.when((d - z) * step > 0)
        def _():
            begins = z == (0 if step > 0 else n - 1)

            @pl.when(jnp.logical_not(begins))
            def _():
                remote(mine, landing.at[way], send_sem, recv_sem.at[way], tp=z - step).wait_recv()
                mine[...] = (acc[...] + landing[way].astype(jnp.float32)).astype(jnp.bfloat16)

            @pl.when(begins)
            def _():
                mine[...] = acc[...].astype(jnp.bfloat16)

            remote(mine, landing.at[way], send_sem, recv_sem.at[way], tp=z + step).start()


def take_in(z, n, acc, landing, recv_sem):
    for way, begins in ((0, 0), (1, n - 1)):
        @pl.when(z != begins)
        def _():
            other = z - 1 if way == 0 else z + 1
            remote(landing.at[way], landing.at[way], recv_sem.at[way], recv_sem.at[way], tp=other).wait_recv()
            acc[...] += landing[way].astype(jnp.float32)


def project_kernel(
    n_grp, n_seq, n_tp,
    match_ref, x_ref, w_ref, ss_ref, rows_ref, pick_ref,
    akv_ref, ameta_ref,
    wbuf, own, acc, pbuf, rbuf, ssbuf, sstot, kvbuf, stage, mstage, kland, mland,
    local_sem, zs, zr, ps, pr, gs, gr, ds, dr, ss_s, ss_r, ks, kr, ms, mr,
):
    me_g, me_s, me_t = lax.axis_index("grp"), lax.axis_index("seq"), lax.axis_index("tp")
    owners = n_grp * n_seq
    me_o = me_g * n_seq + me_s
    features = x_ref.shape[1]
    part = features // owners
    groups = x_ref.shape[0] // GT
    width = rbuf.shape[-1]
    chunks = w_ref.shape[1] // width
    cols = [slice(c * width, (c + 1) * width) for c in range(chunks)]
    waits = []

    def rows_of(g, s):
        return pl.ds(pl.multiple_of((g * n_seq + s) * part, part), part)

    local = pltpu.make_async_copy(
        w_ref.at[pl.ds(pl.multiple_of(me_t * features, features), features), :], wbuf.at[me_t], local_sem
    )
    local.start()

    barrier = pltpu.get_barrier_semaphore()
    for k in range(1, n_tp):
        pl.semaphore_signal(barrier, inc=1, device_id={"tp": lax.rem(me_t + k, n_tp)}, device_id_type=MESH)
    for j in range(1, owners):
        o = lax.rem(me_o + j, owners)
        pl.semaphore_signal(
            barrier, inc=1, device_id={"grp": o // n_seq, "seq": lax.rem(o, n_seq)}, device_id_type=MESH
        )
    pl.semaphore_wait(barrier, n_tp - 1 + owners - 1)

    def w_sends(c):
        copies = []
        for k in range(1, n_tp):
            t = lax.rem(me_t + k, n_tp)
            first = pl.multiple_of(t * features + me_o * part, part)
            copies.append(remote(
                w_ref.at[pl.ds(first, part), cols[c]], wbuf.at[me_t, rows_of(me_g, me_s), cols[c]],
                zs.at[c, k], zr.at[c, k], tp=t,
            ))
            copies[-1].start()
        return copies

    w_copies = [w_sends(0)]
    ss_copies = []
    for k in range(1, n_tp):
        copy = remote(ss_ref, ssbuf.at[k], ss_s.at[k], ss_r.at[k], tp=lax.rem(me_t + k, n_tp))
        copy.start()
        ss_copies.append(copy)

    local.wait()
    own[...] = jnp.dot(x_ref[...], wbuf[me_t], preferred_element_type=jnp.float32)
    for c in range(1, chunks):
        for copy in w_copies[c - 1]:
            copy.wait_send()
        w_copies.append(w_sends(c))
    for copy in w_copies[-1]:
        waits.append(copy)
    waits.extend(ss_copies)

    for c in range(chunks):
        for k in range(1, n_tp):
            t = lax.rem(me_t + n_tp - k, n_tp)
            w_copies[c][k - 1].wait_recv()
            mine = wbuf.at[t, rows_of(me_g, me_s), cols[c]]
            for j in range(1, n_seq):
                copy = remote(mine, mine, ps.at[c, k, j], pr.at[c, k, j], seq=lax.rem(me_s + j, n_seq))
                copy.start()
                waits.append(copy)
            for e in range(1, n_grp):
                copy = remote(mine, mine, gs.at[c, k, 0, e], gr.at[c, k, 0, e], grp=lax.rem(me_g + e, n_grp))
                copy.start()
                waits.append(copy)
    dest_order = sorted(range(n_tp), key=lambda d: (min(d, n_tp - 1 - d), -d))
    for c in range(chunks):
        for k in range(1, n_tp):
            t = lax.rem(me_t + n_tp - k, n_tp)
            for j in range(1, n_seq):
                s = lax.rem(me_s + n_seq - j, n_seq)
                theirs = wbuf.at[t, rows_of(me_g, s), cols[c]]
                remote(theirs, theirs, ps.at[c, k, j], pr.at[c, k, j], seq=s).wait_recv()
                for e in range(1, n_grp):
                    copy = remote(
                        theirs, theirs, gs.at[c, k, j, e], gr.at[c, k, j, e], grp=lax.rem(me_g + e, n_grp)
                    )
                    copy.start()
                    waits.append(copy)
        for d in dest_order:
            k = lax.rem(me_t + n_tp - d, n_tp)

            @pl.when(me_t != d)
            def _():
                for j in range(n_seq):
                    s = lax.rem(me_s + n_seq - j, n_seq)
                    for e in range(1, n_grp):
                        g = lax.rem(me_g + n_grp - e, n_grp)
                        theirs = wbuf.at[d, rows_of(g, s), cols[c]]
                        remote(theirs, theirs, gs.at[c, k, j, e], gr.at[c, k, j, e], grp=g).wait_recv()
                acc[...] = jnp.dot(x_ref[...], wbuf[d, :, cols[c]], preferred_element_type=jnp.float32)
                pass_on(me_t, n_tp, d, acc, pbuf.at[d, c], rbuf.at[:, d, c], ds.at[c, d], dr.at[:, c, d])

    total = ss_ref[...]
    for k in range(1, n_tp):
        ss_copies[k - 1].wait_recv()
        total = total + ssbuf[k]
    sstot[...] = total
    for c in range(chunks):
        acc[...] = own[:, cols[c]]
        take_in(me_t, n_tp, acc, rbuf.at[:, me_t, c], dr.at[:, c, me_t])
        kvbuf[:, cols[c]] = acc[...].astype(jnp.bfloat16)

    out = []
    sub = lax.broadcasted_iota(jnp.int32, (8, 128), 0)
    for j in range(owners):
        o = lax.rem(me_o + j, owners)
        stage[j] = jnp.dot(
            pick_ref[j * GT : (j + 1) * GT], kvbuf[...], preferred_element_type=jnp.float32
        ).astype(jnp.bfloat16)
        sums = match_ref[j, 0] * sstot[0:1, :]
        for i in range(1, groups):
            sums = sums + match_ref[j, i] * sstot[i : i + 1, :]
        mstage[j] = jnp.where(sub == 0, jnp.broadcast_to(sums, (8, 128)), rows_ref[j])
        if j > 0:
            where = dict(grp=o // n_seq, seq=lax.rem(o, n_seq))
            for copy in (
                remote(stage.at[j], kland.at[j], ks.at[j], kr.at[j], **where),
                remote(mstage.at[j], mland.at[j], ms.at[j], mr.at[j], **where),
            ):
                copy.start()
                out.append(copy)
    akv_ref[0] = stage[0]
    ameta_ref[0] = mstage[0]
    for copy in out:
        copy.wait_recv()
    for j in range(1, owners):
        akv_ref[j] = kland[j]
        ameta_ref[j] = mland[j]
    for copy in waits + out:
        copy.wait_send()
    for c in range(chunks):
        for d in range(n_tp):
            @pl.when(me_t != d)
            def _():
                remote(pbuf.at[d, c], rbuf.at[0, d, c], ds.at[c, d], dr.at[0, c, d], tp=d).wait_send()


def attention_kernel(
    kv_heads, head_group, inverse_root,
    lengths_ref, q_ref, new_ref, cache_ref, scale_ref, sent_ref, rms_ref, rows_ref, out_ref,
):
    f32, bf16 = jnp.float32, jnp.bfloat16
    step_rows, context = cache_ref.shape[0], cache_ref.shape[1]
    head_rows = head_group * NEW
    all_rows = step_rows * head_rows
    first = pl.program_id(0) * step_rows
    position = lax.broadcasted_iota(jnp.int32, (head_rows, context), 1)

    def scores(a, b):
        return lax.dot_general(a, b, (((1,), (1,)), ((), ())), preferred_element_type=f32)

    sent_count, new_count = sent_ref.shape[0], step_rows * NEW
    of_row = lax.broadcasted_iota(jnp.int32, (all_rows, sent_count), 0) // head_rows + first
    sent_live = rows_ref[...] == of_row.astype(f32)
    row = lax.broadcasted_iota(jnp.int32, (all_rows, new_count), 0)
    column = lax.broadcasted_iota(jnp.int32, (all_rows, new_count), 1)
    new_live = (column // NEW == row // head_rows) & (column % NEW <= row % NEW)
    for n in range(kv_heads):
        key = slice(n * 2 * HD, n * 2 * HD + HD)
        value = slice(n * 2 * HD + HD, (n + 1) * 2 * HD)
        q = q_ref[n]
        parts = []
        for r in range(step_rows):
            part = scores(q[r * head_rows : (r + 1) * head_rows], cache_ref[r, :, key])
            part = part * scale_ref[n, 0, r : r + 1, :] * inverse_root
            parts.append(jnp.where(position < lengths_ref[first + r], part, -jnp.inf))
        s_cache = jnp.concatenate(parts, axis=0)
        s_sent = scores(q, sent_ref[:, key]) * rms_ref[...] * inverse_root
        s_sent = jnp.where(sent_live, s_sent, -jnp.inf)
        s_new = jnp.where(new_live, scores(q, new_ref[:, key]) * inverse_root, -jnp.inf)
        top = jnp.maximum(
            jnp.maximum(jnp.max(s_cache, axis=1, keepdims=True), jnp.max(s_sent, axis=1, keepdims=True)),
            jnp.max(s_new, axis=1, keepdims=True),
        )
        w_cache, w_sent, w_new = jnp.exp(s_cache - top), jnp.exp(s_sent - top), jnp.exp(s_new - top)
        denominator = (
            jnp.sum(w_cache, axis=1, keepdims=True)
            + jnp.sum(w_sent, axis=1, keepdims=True)
            + jnp.sum(w_new, axis=1, keepdims=True)
        )
        parts = []
        for r in range(step_rows):
            part = w_cache[r * head_rows : (r + 1) * head_rows] * scale_ref[n, 1, r : r + 1, :]
            parts.append(jnp.dot(part.astype(bf16), cache_ref[r, :, value], preferred_element_type=f32))
        total = jnp.concatenate(parts, axis=0)
        total = total + jnp.dot(
            (w_sent * rms_ref[...]).astype(bf16), sent_ref[:, value], preferred_element_type=f32
        )
        total = total + jnp.dot(w_new.astype(bf16), new_ref[:, value], preferred_element_type=f32)
        out_ref[n] = (total / denominator).astype(bf16)


def output_kernel(
    n_seq, n_tp, attn_ref, w_ref, out_ref, wv, held, acc, own, pbuf, rbuf, local_sem, as_, ar, ds, dr
):
    me_s, me_t = lax.axis_index("seq"), lax.axis_index("tp")
    per = n_seq // n_tp
    rows, columns = attn_ref.shape[0], w_ref.shape[1]
    tile = acc.shape[1]
    local = pltpu.make_async_copy(w_ref, wv, local_sem)
    local.start()
    barrier = pltpu.get_barrier_semaphore()
    for k in range(1, n_tp):
        pl.semaphore_signal(barrier, inc=1, device_id={"tp": lax.rem(me_t + k, n_tp)}, device_id_type=MESH)
    for j in range(1, n_seq):
        pl.semaphore_signal(barrier, inc=1, device_id={"seq": lax.rem(me_s + j, n_seq)}, device_id_type=MESH)
    pl.semaphore_wait(barrier, n_tp - 1 + n_seq - 1)

    gathers = []
    for j in range(1, n_seq):
        copy = remote(attn_ref, held.at[j], as_.at[j], ar.at[j], seq=lax.rem(me_s + j, n_seq))
        copy.start()
        gathers.append(copy)
    local.wait()
    for j in range(n_seq):
        s = lax.rem(me_s + n_seq - j, n_seq)
        dest, sub = s // per, lax.rem(s, per)
        if j > 0:
            gathers[j - 1].wait_recv()
        block = attn_ref if j == 0 else held.at[j]

        @pl.loop(0, columns // tile)
        def _(c):
            acc[...] = jnp.dot(
                block[...], wv[:, pl.ds(pl.multiple_of(c * tile, tile), tile)], preferred_element_type=jnp.float32
            )

            @pl.when(dest == me_t)
            def _():
                own[sub, c] = acc[...]

            @pl.when(dest != me_t)
            def _():
                pass_on(me_t, n_tp, dest, acc, pbuf.at[s, c], rbuf.at[:, s, c], ds.at[s, c], dr.at[:, s, c])

    for u in range(per):
        for c in range(columns // tile):
            s = me_t * per + u
            acc[...] = own[u, c]
            take_in(me_t, n_tp, acc, rbuf.at[:, s, c], dr.at[:, s, c])
            out_ref[u * rows : (u + 1) * rows, c * tile : (c + 1) * tile] = acc[...].astype(jnp.bfloat16)
    for copy in gathers:
        copy.wait_send()
    for k in range(1, n_tp):
        t = lax.rem(me_t + k, n_tp)
        for u in range(per):
            s = t * per + u
            for c in range(columns // tile):
                remote(pbuf.at[s, c], rbuf.at[0, s, c], ds.at[s, c], dr.at[0, s, c], tp=t).wait_send()


def on_device(
    prompt, w_kv, block_owner, block_row, queries, new_kv, cache_codes, cache_scales, lengths, w_out
):
    n_grp, n_seq, n_tp = lax.axis_size("grp"), lax.axis_size("seq"), lax.axis_size("tp")
    owners = n_grp * n_seq
    tokens, features = prompt.shape
    columns = w_kv.shape[1]
    row_count = queries.shape[0]
    groups = tokens // GT

    group_owner = block_owner[:, 0].reshape(groups, CAP)[:, 0]
    group_row = block_row.reshape(groups, CAP)[:, 0]
    me_o = lax.axis_index("grp") * n_seq + lax.axis_index("seq")
    order = (me_o + jnp.arange(owners, dtype=jnp.int32)) % owners
    match = group_owner[None, :] == order[:, None]
    token_of = jnp.arange(owners * GT)[:, None] % GT == jnp.arange(tokens)[None, :] % GT
    pick = jnp.repeat(jnp.repeat(match, GT, axis=0), GT, axis=1) & token_of
    send_row = jnp.sum(jnp.where(match, group_row[None, :] + 1, 0), axis=1) - 1
    row_tiles = jnp.broadcast_to(send_row.astype(jnp.float32)[:, None, None], (owners, 8, 128))
    widened = prompt.astype(jnp.float32)
    squares = jnp.sum(widened * widened, axis=1).reshape(groups, GT)
    squares = jnp.pad(squares, ((0, -groups % 8), (0, 128 - GT)))

    width = min(256, columns)
    chunks = columns // width
    dma = pltpu.SemaphoreType.DMA
    vmem = pl.BlockSpec(memory_space=pltpu.VMEM)
    bf16, f32 = jnp.bfloat16, jnp.float32
    arrived, meta = pl.pallas_call(
        functools.partial(project_kernel, n_grp, n_seq, n_tp),
        out_shape=(
            jax.ShapeDtypeStruct((owners, GT, columns), bf16),
            jax.ShapeDtypeStruct((owners, 8, 128), f32),
        ),
        in_specs=[
            pl.BlockSpec(memory_space=pltpu.SMEM), vmem, pl.BlockSpec(memory_space=pl.ANY), vmem, vmem, vmem,
        ],
        out_specs=(vmem, vmem),
        scratch_shapes=[
            pltpu.VMEM((n_tp, features, columns), bf16),
            pltpu.VMEM((tokens, columns), f32),
            pltpu.VMEM((tokens, width), f32),
            pltpu.VMEM((n_tp, chunks, tokens, width), bf16),
            pltpu.VMEM((2, n_tp, chunks, tokens, width), bf16),
            pltpu.VMEM((n_tp,) + squares.shape, f32),
            pltpu.VMEM(squares.shape, f32),
            pltpu.VMEM((tokens, columns), bf16),
            pltpu.VMEM((owners, GT, columns), bf16),
            pltpu.VMEM((owners, 8, 128), f32),
            pltpu.VMEM((owners, GT, columns), bf16),
            pltpu.VMEM((owners, 8, 128), f32),
            dma, dma((chunks, n_tp)), dma((chunks, n_tp)),
            dma((chunks, n_tp, n_seq)), dma((chunks, n_tp, n_seq)),
            dma((chunks, n_tp, n_seq, n_grp)), dma((chunks, n_tp, n_seq, n_grp)),
            dma((chunks, n_tp)), dma((2, chunks, n_tp)), dma((n_tp,)), dma((n_tp,)),
            dma((owners,)), dma((owners,)), dma((owners,)), dma((owners,)),
        ],
        compiler_params=pltpu.CompilerParams(
            collective_id=0, has_side_effects=True, vmem_limit_bytes=48 * MIB
        ),
        cost_estimate=pl.CostEstimate(
            flops=2 * tokens * features * columns * n_tp, bytes_accessed=16 * MIB, transcendentals=0
        ),
    )(match.astype(f32), prompt, w_kv, squares, row_tiles, pick.astype(bf16))

    kv_heads = columns // (2 * HD)
    head_group = HQ // KVH
    context = cache_codes.shape[1]
    inverse_root = 1.0 / math.sqrt(HD)
    head_rows = head_group * NEW
    query_heads = jnp.transpose(
        queries.reshape(row_count, NEW, kv_heads, head_group, HD), (2, 0, 3, 1, 4)
    ).reshape(kv_heads, row_count * head_rows, HD)
    block_scales = jnp.transpose(
        cache_scales.reshape(row_count, context // CBLK, kv_heads, 2), (2, 3, 0, 1)
    )
    scales = jnp.repeat(block_scales, CBLK, axis=3)
    sent_rms = lax.rsqrt(meta[:, 0, :GT].reshape(1, owners * GT) / (features * n_tp) + EPS)
    sent_rows = jnp.repeat(meta[:, 1, 0], GT)[None, :]
    step_rows = 8
    attention = pl.pallas_call(
        functools.partial(attention_kernel, kv_heads, head_group, inverse_root),
        grid=(row_count // step_rows,),
        out_shape=jax.ShapeDtypeStruct((kv_heads, row_count * head_rows, HD), bf16),
        in_specs=[
            pl.BlockSpec(memory_space=pltpu.SMEM),
            pl.BlockSpec((kv_heads, step_rows * head_rows, HD), lambda i: (0, i, 0)),
            pl.BlockSpec((step_rows * NEW, columns), lambda i: (i, 0)),
            pl.BlockSpec((step_rows, context, columns), lambda i: (i, 0, 0)),
            pl.BlockSpec((kv_heads, 2, step_rows, context), lambda i: (0, 0, i, 0)),
            pl.BlockSpec((owners * GT, columns), lambda i: (0, 0)),
            pl.BlockSpec((1, owners * GT), lambda i: (0, 0)),
            pl.BlockSpec((1, owners * GT), lambda i: (0, 0)),
        ],
        out_specs=pl.BlockSpec((kv_heads, step_rows * head_rows, HD), lambda i: (0, i, 0)),
        compiler_params=pltpu.CompilerParams(vmem_limit_bytes=32 * MIB),
        cost_estimate=pl.CostEstimate(
            flops=4 * row_count * head_rows * kv_heads * HD * (context + owners * GT),
            bytes_accessed=8 * MIB, transcendentals=0,
        ),
    )(
        lengths, query_heads, new_kv.reshape(row_count * NEW, columns), cache_codes, scales,
        arrived.reshape(owners * GT, columns), sent_rms, sent_rows,
    )
    attention = jnp.transpose(
        attention.reshape(kv_heads, row_count, head_group, NEW, HD), (1, 3, 0, 2, 4)
    ).reshape(row_count * NEW, kv_heads * head_group * HD)
    rows, depth = attention.shape
    per = n_seq // n_tp
    out_columns = w_out.shape[1]
    tile = min(1024, out_columns)
    tiles = out_columns // tile
    return pl.pallas_call(
        functools.partial(output_kernel, n_seq, n_tp),
        out_shape=jax.ShapeDtypeStruct((per * rows, out_columns), bf16),
        in_specs=[vmem, pl.BlockSpec(memory_space=pl.ANY)],
        out_specs=vmem,
        scratch_shapes=[
            pltpu.VMEM((depth, out_columns), bf16),
            pltpu.VMEM((n_seq, rows, depth), bf16),
            pltpu.VMEM((rows, tile), f32),
            pltpu.VMEM((per, tiles, rows, tile), f32),
            pltpu.VMEM((n_seq, tiles, rows, tile), bf16),
            pltpu.VMEM((2, n_seq, tiles, rows, tile), bf16),
            dma, dma((n_seq,)), dma((n_seq,)), dma((n_seq, tiles)), dma((2, n_seq, tiles)),
        ],
        compiler_params=pltpu.CompilerParams(
            collective_id=1, has_side_effects=True, vmem_limit_bytes=48 * MIB
        ),
        cost_estimate=pl.CostEstimate(
            flops=2 * rows * n_seq * depth * out_columns, bytes_accessed=16 * MIB, transcendentals=0
        ),
    )(attention, w_out)


def solution(mesh):
    in_specs = (
        P(("grp", "seq"), "tp"),
        P(None, "tp"),
        P(("grp", "seq"), None),
        P(("grp", "seq")),
        P(("grp", "seq"), None, "tp"),
        P(("grp", "seq"), None, "tp"),
        P(("grp", "seq"), None, "tp"),
        P(("grp", "seq"), None, "tp"),
        P(("grp", "seq")),
        P("tp", "seq"),
    )
    out_specs = P(("grp", "tp"), "seq")
    return jax.shard_map(
        on_device, mesh=mesh, in_specs=in_specs, out_specs=out_specs, check_vma=False
    )
```
